32 devices in a mesh: cp: 16 (over z, x, core), hd: 2 (over y).
Axes of the slice: x: 2, y: 2, z: 4, core: 2. Of those that a mesh axis runs over, the one named last changes fastest.
Arguments:
- query: bfloat16 [8192, 512], P('cp', 'hd'), may hold values from -6 to 6
- keys: bfloat16 [8192, 128], P('cp'), may hold values from -4 to 4
- values: bfloat16 [8192, 128], P('cp'), may hold values from -4 to 6
- grad_out: bfloat16 [8192, 512], P('cp', 'hd'), may hold values from -6 to 6
- doc_start: int32 [8192], P('cp'), may hold values from 0 to 8191, as said below
Outputs:
- grad_query: bfloat16 [8192, 512], P('cp', 'hd')
- grad_keys: bfloat16 [8192, 128], P('cp')
- grad_values: bfloat16 [8192, 128], P('cp')
The draws below stay inside these ranges and needn't reach their ends.
Inputs may be any that keep to these rules, and one draw needn't show every extreme that they name: `doc_start`: documents are contiguous runs of tokens of at most 4096 tokens; no document crosses a multiple of 4096 tokens; the first 4096 tokens form one document; the last token forms a document of its own.
All inputs are finite; a program needn't handle non-finite values.
Results may differ from the reference program's by a relative error of at most 0.0075.
Values may be sent and summed in bfloat16 or wider, within the bound.
A program may use at most 64 MiB of HBM per device.

```python
import math
import jax
import jax.numpy as jnp
from jax import lax

HEADS = 4
HDIM = 128
TOK_DEV = 512
SPAN = 8
MAXDOC = 4096
TOKENS = 8192
N_CP = 16


def draw_query(key, part):
    key = jax.random.fold_in(key, 11)
    drawn = jnp.clip(jax.random.normal(key, (TOKENS, HEADS * HDIM), jnp.float32), -4.0, 4.0)
    return drawn.astype(jnp.bfloat16)


def draw_keys(key, part):
    key = jax.random.fold_in(key, 12)
    noise_key, scale_key = jax.random.split(key)
    block_scale = jnp.exp(jax.random.uniform(scale_key, (TOKENS // TOK_DEV,), jnp.float32, -0.7, 0.5))
    row_scale = block_scale[jnp.arange(TOKENS) // TOK_DEV]
    drawn = jnp.clip(jax.random.normal(noise_key, (TOKENS, HDIM), jnp.float32) * row_scale[:, None], -4.0, 4.0)
    return drawn.astype(jnp.bfloat16)


def draw_values(key, part):
    key = jax.random.fold_in(key, 14)
    noise_key, shift_key = jax.random.split(key)
    column_shift = jax.random.uniform(shift_key, (HDIM,), jnp.float32, 0.5, 1.5)
    noise = jnp.clip(jax.random.normal(noise_key, (TOKENS, HDIM), jnp.float32), -4.0, 4.0)
    return (noise + column_shift[None, :]).astype(jnp.bfloat16)


def draw_doc_start(key, part):
    key = jax.random.fold_in(key, 13)
    rate_key, token_key, forced_key = jax.random.split(key, 3)
    positions = jnp.arange(TOKENS, dtype=jnp.int32)
    block_index = positions // MAXDOC
    rate_bits = jax.random.randint(rate_key, (TOKENS // MAXDOC,), 3, 13)
    token_bits = rate_bits[block_index]
    tosses = jax.random.randint(token_key, (TOKENS,), 0, 4096)
    forced_pos = jax.random.randint(forced_key, (TOKENS // MAXDOC,), 1, MAXDOC)
    boundary = (tosses < 4096 >> token_bits) & (block_index > 0)
    boundary = boundary | (positions % MAXDOC == forced_pos[block_index]) & (block_index > 0)
    boundary = boundary | (positions % MAXDOC == 0) | (positions == TOKENS - 1)
    starts = jnp.where(boundary, positions, 0)
    return lax.cummax(starts, axis=0).astype(jnp.int32)


def steps_of(key, shape, shards, smallest, largest):
    level = 1.0
    for position, blocks in shards:
        draws = jax.random.uniform(jax.random.fold_in(jax.random.fold_in(key, 6), position), (blocks,), jnp.float32, smallest / len(shards), largest / len(shards))
        level = level * jnp.repeat(jnp.exp(draws), shape[position] // blocks).reshape((-1,) + (1,) * (len(shape) - 1 - position))
    return level


def normal_values(own_key, extent, deviation, bound, pieces=(), kind=jnp.bfloat16):
    factor_of = steps_of(own_key, extent, pieces, -0.22, 0.18) if pieces else 1.0
    entries = jax.random.normal(own_key, extent, jnp.float32) * deviation * factor_of
    return jnp.minimum(jnp.maximum(entries, -bound), bound).astype(kind)


def setup_inputs(seed: int = 0) -> dict:
    splits = jax.random.split(jax.random.key(seed), 6)
    query = draw_query(jax.random.fold_in(splits[5], 71), 0)
    keys = draw_keys(jax.random.fold_in(splits[5], 71), 0)
    values = draw_values(jax.random.fold_in(splits[5], 71), 0)
    grad_out = normal_values(splits[3], (TOKENS, HEADS * HDIM), 1.0, 6.0, ((0, 16), (1, 2)))
    doc_start = draw_doc_start(jax.random.fold_in(splits[5], 71), 0)
    return dict(query=query, keys=keys, values=values, grad_out=grad_out, doc_start=doc_start)


masked_score = -1e+30

def low_round(tensor):
    return lax.optimization_barrier(tensor.astype(jnp.bfloat16)).astype(jnp.float32)

def reference(query, keys, values, grad_out, doc_start):
    scaling = 1.0 / math.sqrt(HDIM)
    lookback = (SPAN - 1) * TOK_DEV
    window = SPAN * TOK_DEV
    query_heads = query.reshape(TOKENS, HEADS, HDIM)
    grad_heads = grad_out.reshape(TOKENS, HEADS, HDIM)
    keys_padded = jnp.concatenate([jnp.zeros((lookback, HDIM), keys.dtype), keys], 0)
    values_padded = jnp.concatenate([jnp.zeros((lookback, HDIM), values.dtype), values], 0)

    def one_block(carried, block):
        key_grad, value_grad = carried
        first = (block * TOK_DEV).astype(jnp.int32)
        query_part = lax.dynamic_slice_in_dim(query_heads, first, TOK_DEV, 0).astype(jnp.float32)
        grad_part = lax.dynamic_slice_in_dim(grad_heads, first, TOK_DEV, 0).astype(jnp.float32)
        key_part = lax.dynamic_slice_in_dim(keys_padded, first, window, 0).astype(jnp.float32)
        value_part = lax.dynamic_slice_in_dim(values_padded, first, window, 0).astype(jnp.float32)
        starts = lax.dynamic_slice_in_dim(doc_start, first, TOK_DEV, 0).astype(jnp.int32)
        query_pos = first + jnp.arange(TOK_DEV, dtype=jnp.int32)
        key_pos = first - lookback + jnp.arange(window, dtype=jnp.int32)
        allowed = (key_pos[None, :] >= starts[:, None]) & (key_pos[None, :] <= query_pos[:, None])
        scores = jnp.einsum('thd,kd->htk', query_part, key_part) * scaling
        scores = jnp.where(allowed[None], scores, masked_score)
        row_max = lax.optimization_barrier(jnp.max(scores, axis=-1, keepdims=True))
        log_norm = row_max + jnp.log(lax.optimization_barrier(jnp.sum(jnp.exp(scores - row_max), axis=-1, keepdims=True)))
        probs = jnp.where(allowed[None], jnp.exp(scores - log_norm), 0.0)
        grad_prob = jnp.einsum('thd,kd->htk', grad_part, value_part)
        row_delta = lax.optimization_barrier(jnp.sum(probs * grad_prob, axis=-1, keepdims=True))
        grad_score = low_round(probs * (grad_prob - row_delta))
        probs_low = low_round(probs)
        grad_query = (jnp.einsum('htk,kd->thd', grad_score, key_part) * scaling).astype(jnp.bfloat16)
        key_term = jnp.einsum('htk,thd->kd', grad_score, query_part) * scaling
        value_term = jnp.einsum('htk,thd->kd', probs_low, grad_part)
        key_grad = lax.dynamic_update_slice_in_dim(key_grad, lax.dynamic_slice_in_dim(key_grad, first, window, 0) + key_term, first, 0)
        value_grad = lax.dynamic_update_slice_in_dim(value_grad, lax.dynamic_slice_in_dim(value_grad, first, window, 0) + value_term, first, 0)
        return ((key_grad, value_grad), grad_query.reshape(TOK_DEV, HEADS * HDIM))
    start_grads = (jnp.zeros((TOKENS + lookback, HDIM), jnp.float32), jnp.zeros((TOKENS + lookback, HDIM), jnp.float32))
    (key_grad, value_grad), query_blocks = lax.scan(one_block, start_grads, jnp.arange(N_CP, dtype=jnp.int32))
    grad_query = query_blocks.reshape(TOKENS, HEADS * HDIM)
    grad_keys = key_grad[lookback:].astype(jnp.bfloat16)
    grad_values = value_grad[lookback:].astype(jnp.bfloat16)
    return (grad_query, grad_keys, grad_values)
```

```python
import functools
import math

import jax
import jax.numpy as jnp
from jax import lax
from jax.experimental import pallas as pl
from jax.experimental.pallas import tpu as pltpu
from jax.sharding import PartitionSpec as P

HDIM = 128
MAXDOC = 4096
MESH = pl.DeviceIdType.MESH
BF16 = jnp.bfloat16
F32 = jnp.float32
MASKED = -1e30


def xor3(a, b):
    out = 0
    for bit in (1, 2, 4):
        x, y = (a // bit) % 2, (b // bit) % 2
        out = out + bit * (x + y - 2 * x * y)
    return out


def dot(a, b, contract=((1,), (0,))):
    return lax.dot_general(a, b, (contract, ((), ())), preferred_element_type=F32)


def kernel(
    span,
    q_ref, k_ref, v_ref, do_ref, start_ref,
    dq_ref, dk_ref, dv_ref,
    kv, qs, dos, qt, dot_t, e_all, d_all, m_all, m_run, l_run, w_run, dq_t, acc,
    sib_out, sib_in, red_out, red_in, hd_out, hd_in,
    kv_send, kv_recv, sib_send, sib_recv, red_send, red_recv, hd_sem,
):
    rows = k_ref.shape[0]
    heads = q_ref.shape[1] // HDIM
    wide = heads * rows
    chunk = rows // 2
    tile = rows // 2
    scaling = 1.0 / math.sqrt(HDIM)
    scale2 = scaling * math.log2(math.e)

    pos = lax.axis_index("cp")
    me = pos % span
    base = pos - me
    twin = {"hd": 1 - lax.axis_index("hd")}

    def peer(index):
        return {"cp": base + index}

    sibling = xor3(me, 1)
    partners = [xor3(me, 2 * d) for d in range(1, span // 2)]

    barrier = pltpu.get_barrier_semaphore()
    for other in [peer(sibling)] + [peer(p) for p in partners] + [twin]:
        pl.semaphore_signal(barrier, inc=1, device_id=other, device_id_type=MESH)
    pl.semaphore_wait(barrier, 2 + len(partners))

    def remote(src, dst, send, recv, device):
        return pltpu.make_async_remote_copy(
            src_ref=src, dst_ref=dst, send_sem=send, recv_sem=recv,
            device_id=device, device_id_type=MESH,
        )

    def own_copy(d, target):
        return remote(kv.at[me], kv.at[me], kv_send.at[d], kv_recv.at[me], peer(target))

    def relay_copy(d, slot):
        return remote(
            kv.at[slot], kv.at[slot], kv_send.at[span // 2 + d], kv_recv.at[slot], peer(sibling)
        )

    def sib_copy(d):
        return remote(
            sib_out.at[d], sib_in.at[d], sib_send.at[d], sib_recv.at[d], peer(sibling)
        )

    def red_copy(d, target):
        return remote(
            red_out.at[d], red_in.at[d], red_send.at[d], red_recv.at[d], peer(target)
        )

    kv[me, 0] = k_ref[...]
    kv[me, 1] = v_ref[...]
    for d, target in enumerate(partners, 1):
        @pl.when(target > me)
        def _():
            own_copy(d, target).start()

    @pl.when(sibling > me)
    def _():
        own_copy(0, sibling).start()

    for h in range(heads):
        at = slice(h * rows, (h + 1) * rows)
        q = q_ref[:, h * HDIM:(h + 1) * HDIM]
        g = do_ref[:, h * HDIM:(h + 1) * HDIM]
        qs[at, :] = q
        dos[at, :] = g
        qt[:, at] = q.T
        dot_t[:, at] = g.T
    m_run[...] = jnp.full_like(m_run, MASKED)
    l_run[...] = jnp.zeros_like(l_run)
    w_run[...] = jnp.zeros_like(w_run)
    dq_t[...] = jnp.zeros_like(dq_t)

    def stat_tile(s, kc, tq, diagonal):
        at_k = slice(kc * chunk, (kc + 1) * chunk)
        at_q = slice(tq * tile, (tq + 1) * tile)
        row0 = (tq * tile) % rows
        scores = dot(kv[s, 0, at_k, :], qt[:, at_q]) * scale2
        grad_prob = dot(kv[s, 1, at_k, :], dot_t[:, at_q])
        key_pos = lax.broadcasted_iota(jnp.int32, (chunk, tile), 0)
        first = start_ref[:, row0:row0 + tile] - ((base + s) * rows + kc * chunk)
        allowed = key_pos >= first
        if diagonal:
            query_pos = lax.broadcasted_iota(jnp.int32, (chunk, tile), 1) + (row0 - kc * chunk)
            allowed = allowed & (key_pos <= query_pos)
        scores = jnp.where(allowed, scores, MASKED)
        old = m_run[:, at_q]
        new = jnp.maximum(old, jnp.max(scores, axis=0, keepdims=True))
        e = jnp.exp2(scores - new)
        fac = jnp.exp2(old - new)
        l_run[:, at_q] = l_run[:, at_q] * fac + jnp.sum(e, axis=0, keepdims=True)
        w_run[:, at_q] = w_run[:, at_q] * fac + jnp.sum(e * grad_prob, axis=0, keepdims=True)
        m_run[:, at_q] = new
        m_all[s, kc, :, at_q] = new
        e_all[s, at_k, at_q] = e
        d_all[s, at_k, at_q] = grad_prob

    for tq in range(wide // tile):
        first_kc = tq % (rows // tile)
        for kc in (first_kc, 1 - first_kc):
            stat_tile(me, kc, tq, True)

    def stat_step(t, _):
        s = xor3(me, t)

        @pl.when(s < me)
        def _():
            relay_copy(0, s).wait_recv()

            @pl.when(t % 2 == 0)
            def _():
                relay_copy(t // 2, s).start()

            for tq in range(wide // tile):
                for kc in range(rows // chunk):
                    stat_tile(s, kc, tq, False)

        return 0

    lax.fori_loop(1, span, stat_step, 0)

    inv = 1.0 / l_run[...]
    l_run[...] = inv
    w_run[...] = w_run[...] * inv

    def grad_step(i, _):
        t = span - 1 - i
        s = xor3(me, t)
        d = t // 2

        @pl.when(s <= me)
        def _():
            delta = w_run[...]
            for kc in range(rows // chunk):
                at_k = slice(kc * chunk, (kc + 1) * chunk)
                fac = jnp.exp2(m_all[s, kc] - m_run[...]) * l_run[...]
                p = e_all[s, at_k, :] * fac
                ds = (p * (d_all[s, at_k, :] - delta)).astype(BF16)
                acc[0, at_k, :] = dot(ds, qs[...])
                acc[1, at_k, :] = dot(p.astype(BF16), dos[...])
                dq_t[...] += dot(kv[s, 0, at_k, :], ds, ((0,), (0,)))

            @pl.when(t % 2 == 1)
            def _():
                sib_out[d] = acc[...].astype(BF16)
                sib_copy(d).start()

            @pl.when((t % 2 == 0) & (t > 0))
            def _():
                sib_copy(d).wait_recv()
                red_out[d] = (acc[...] + sib_in[d].astype(F32)).astype(BF16)
                red_copy(d, s).start()

        return 0

    lax.fori_loop(0, span, grad_step, 0)

    for h in range(heads):
        dq_ref[:, h * HDIM:(h + 1) * HDIM] = (
            (dq_t[:, h * rows:(h + 1) * rows] * scaling).T.astype(BF16)
        )

    @pl.when(sibling > me)
    def _():
        sib_copy(0).wait_recv()
        acc[...] += sib_in[0].astype(F32)

    for d, target in enumerate(partners, 1):
        @pl.when(target > me)
        def _():
            red_copy(d, target).wait_recv()
            acc[...] += red_in[d].astype(F32)

    hd_out[...] = acc[...].astype(BF16)
    hd_copy = remote(hd_out, hd_in, hd_sem.at[0], hd_sem.at[1], twin)
    hd_copy.start()
    hd_copy.wait()
    dk_ref[...] = ((hd_out[0].astype(F32) + hd_in[0].astype(F32)) * scaling).astype(BF16)
    dv_ref[...] = (hd_out[1].astype(F32) + hd_in[1].astype(F32)).astype(BF16)

    @pl.when(sibling > me)
    def _():
        own_copy(0, sibling).wait_send()

    @pl.when(sibling < me)
    def _():
        sib_copy(0).wait_send()

    for d, target in enumerate(partners, 1):
        @pl.when(target > me)
        def _():
            own_copy(d, target).wait_send()

        @pl.when(target < me)
        def _():
            relay_copy(d, target).wait_send()
            sib_copy(d).wait_send()
            red_copy(d, target).wait_send()


def body(query, keys, values, grad_out, doc_start):
    rows = keys.shape[0]
    heads = query.shape[1] // HDIM
    wide = heads * rows
    span = MAXDOC // rows
    vmem = pl.BlockSpec(memory_space=pltpu.VMEM)
    pair = (2, rows, HDIM)
    return pl.pallas_call(
        functools.partial(kernel, span),
        out_shape=(
            jax.ShapeDtypeStruct(query.shape, BF16),
            jax.ShapeDtypeStruct(keys.shape, BF16),
            jax.ShapeDtypeStruct(values.shape, BF16),
        ),
        in_specs=[vmem] * 5,
        out_specs=(vmem,) * 3,
        scratch_shapes=[
            pltpu.VMEM((span,) + pair, BF16),
            pltpu.VMEM((wide, HDIM), BF16),
            pltpu.VMEM((wide, HDIM), BF16),
            pltpu.VMEM((HDIM, wide), BF16),
            pltpu.VMEM((HDIM, wide), BF16),
            pltpu.VMEM((span, rows, wide), F32),
            pltpu.VMEM((span, rows, wide), F32),
            pltpu.VMEM((span, 2, 1, wide), F32),
            pltpu.VMEM((1, wide), F32),
            pltpu.VMEM((1, wide), F32),
            pltpu.VMEM((1, wide), F32),
            pltpu.VMEM((HDIM, wide), F32),
            pltpu.VMEM(pair, F32),
            pltpu.VMEM((span // 2,) + pair, BF16),
            pltpu.VMEM((span // 2,) + pair, BF16),
            pltpu.VMEM((span // 2,) + pair, BF16),
            pltpu.VMEM((span // 2,) + pair, BF16),
            pltpu.VMEM(pair, BF16),
            pltpu.VMEM(pair, BF16),
            pltpu.SemaphoreType.DMA((span,)),
            pltpu.SemaphoreType.DMA((span,)),
            pltpu.SemaphoreType.DMA((span // 2,)),
            pltpu.SemaphoreType.DMA((span // 2,)),
            pltpu.SemaphoreType.DMA((span // 2,)),
            pltpu.SemaphoreType.DMA((span // 2,)),
            pltpu.SemaphoreType.DMA((2,)),
        ],
        compiler_params=pltpu.CompilerParams(
            collective_id=0, has_side_effects=True, vmem_limit_bytes=56 * 1024 * 1024
        ),
    )(query, keys, values, grad_out, doc_start.reshape(1, rows))


def solution(mesh):
    in_specs = (P("cp", "hd"), P("cp", None), P("cp", None), P("cp", "hd"), P("cp"))
    out_specs = (P("cp", "hd"), P("cp", None), P("cp", None))
    return jax.shard_map(body, mesh=mesh, in_specs=in_specs, out_specs=out_specs, check_vma=False)
```

```python
import functools
import math

import jax
import jax.numpy as jnp
from jax import lax
from jax.experimental import pallas as pl
from jax.experimental.pallas import tpu as pltpu
from jax.sharding import PartitionSpec as P

HDIM = 128
MAXDOC = 4096
MESH = pl.DeviceIdType.MESH
BF16 = jnp.bfloat16
F32 = jnp.float32
MASKED = -1e30


def xor3(a, b):
    out = 0
    for bit in (1, 2, 4):
        x, y = (a // bit) % 2, (b // bit) % 2
        out = out + bit * (x + y - 2 * x * y)
    return out


def dot(a, b, contract=((1,), (0,))):
    return lax.dot_general(a, b, (contract, ((), ())), preferred_element_type=F32)


def kernel(
    span,
    q_ref, k_ref, v_ref, do_ref, start_ref,
    dq_ref, dk_ref, dv_ref,
    kv, qs, dos, qt, dot_t, e_all, d_all, m_all, m_run, l_run, w_run, dq_t, acc,
    sib_out, sib_in, red_out, red_in, hd_out, hd_in,
    kv_send, kv_recv, sib_send, sib_recv, red_send, red_recv, hd_sem,
):
    rows = k_ref.shape[0]
    heads = q_ref.shape[1] // HDIM
    wide = heads * rows
    chunk = rows // 2
    tile = rows // 2
    scaling = 1.0 / math.sqrt(HDIM)
    scale2 = scaling * math.log2(math.e)

    pos = lax.axis_index("cp")
    me = pos % span
    base = pos - me
    side = lax.axis_index("hd")
    twin = {"hd": 1 - side}

    def peer(index, hd=None):
        return {"cp": base + index} if hd is None else {"cp": base + index, "hd": hd}

    sibling = xor3(me, 1)
    partners = [xor3(me, 2 * d) for d in range(1, span // 2)]

    barrier = pltpu.get_barrier_semaphore()
    for other in [peer(sibling), twin] + [peer(p, hd) for p in partners for hd in (0, 1)]:
        pl.semaphore_signal(barrier, inc=1, device_id=other, device_id_type=MESH)
    pl.semaphore_wait(barrier, 2 + 2 * len(partners))

    def remote(src, dst, send, recv, device):
        return pltpu.make_async_remote_copy(
            src_ref=src, dst_ref=dst, send_sem=send, recv_sem=recv,
            device_id=device, device_id_type=MESH,
        )

    def own_copy(d, target):
        return remote(kv.at[me], kv.at[me], kv_send.at[d], kv_recv.at[me], peer(target))

    def relay_copy(d, slot):
        return remote(
            kv.at[slot], kv.at[slot], kv_send.at[span // 2 + d], kv_recv.at[slot], peer(sibling)
        )

    def sib_copy(d):
        return remote(
            sib_out.at[d], sib_in.at[d], sib_send.at[d], sib_recv.at[d], peer(sibling)
        )

    def red_copy(d, part, target):
        return remote(
            red_out.at[d, part], red_in.at[d, side], red_send.at[d, part],
            red_recv.at[d, side], peer(target, part),
        )

    def red_arrival(d, source):
        return remote(
            red_out.at[d, 0], red_in.at[d, source], red_send.at[d, 0],
            red_recv.at[d, source], twin,
        )

    kv[me, 0] = k_ref[...]
    kv[me, 1] = v_ref[...]
    for d, target in enumerate(partners, 1):
        @pl.when(target > me)
        def _():
            own_copy(d, target).start()

    @pl.when(sibling > me)
    def _():
        own_copy(0, sibling).start()

    for h in range(heads):
        at = slice(h * rows, (h + 1) * rows)
        q = q_ref[:, h * HDIM:(h + 1) * HDIM]
        g = do_ref[:, h * HDIM:(h + 1) * HDIM]
        qs[at, :] = q
        dos[at, :] = g
        qt[:, at] = q.T
        dot_t[:, at] = g.T
    m_run[...] = jnp.full_like(m_run, MASKED)
    l_run[...] = jnp.zeros_like(l_run)
    w_run[...] = jnp.zeros_like(w_run)
    dq_t[...] = jnp.zeros_like(dq_t)

    def stat_tile(s, kc, tq, diagonal):
        at_k = slice(kc * chunk, (kc + 1) * chunk)
        at_q = slice(tq * tile, (tq + 1) * tile)
        row0 = (tq * tile) % rows
        scores = dot(kv[s, 0, at_k, :], qt[:, at_q]) * scale2
        grad_prob = dot(kv[s, 1, at_k, :], dot_t[:, at_q])
        key_pos = lax.broadcasted_iota(jnp.int32, (chunk, tile), 0)
        first = start_ref[:, row0:row0 + tile] - ((base + s) * rows + kc * chunk)
        allowed = key_pos >= first
        if diagonal:
            query_pos = lax.broadcasted_iota(jnp.int32, (chunk, tile), 1) + (row0 - kc * chunk)
            allowed = allowed & (key_pos <= query_pos)
        scores = jnp.where(allowed, scores, MASKED)
        old = m_run[:, at_q]
        new = jnp.maximum(old, jnp.max(scores, axis=0, keepdims=True))
        e = jnp.exp2(scores - new)
        fac = jnp.exp2(old - new)
        l_run[:, at_q] = l_run[:, at_q] * fac + jnp.sum(e, axis=0, keepdims=True)
        w_run[:, at_q] = w_run[:, at_q] * fac + jnp.sum(e * grad_prob, axis=0, keepdims=True)
        m_run[:, at_q] = new
        m_all[s, kc, :, at_q] = new
        e_all[s, at_k, at_q] = e
        d_all[s, at_k, at_q] = grad_prob

    for tq in range(wide // tile):
        first_kc = tq % (rows // tile)
        for kc in (first_kc, 1 - first_kc):
            stat_tile(me, kc, tq, True)

    def stat_step(t, _):
        s = xor3(me, t)

        @pl.when(s < me)
        def _():
            relay_copy(0, s).wait_recv()

            @pl.when(t % 2 == 0)
            def _():
                relay_copy(t // 2, s).start()

            for tq in range(wide // tile):
                for kc in range(rows // chunk):
                    stat_tile(s, kc, tq, False)

        return 0

    lax.fori_loop(1, span, stat_step, 0)

    inv = 1.0 / l_run[...]
    l_run[...] = inv
    w_run[...] = w_run[...] * inv

    def grad_step(i, _):
        t = span - 1 - i
        s = xor3(me, t)
        d = t // 2

        @pl.when(s <= me)
        def _():
            delta = w_run[...]
            for kc in range(rows // chunk):
                at_k = slice(kc * chunk, (kc + 1) * chunk)
                fac = jnp.exp2(m_all[s, kc] - m_run[...]) * l_run[...]
                p = e_all[s, at_k, :] * fac
                ds = (p * (d_all[s, at_k, :] - delta)).astype(BF16)
                acc[0, at_k, :] = dot(ds, qs[...])
                acc[1, at_k, :] = dot(p.astype(BF16), dos[...])
                dq_t[...] += dot(kv[s, 0, at_k, :], ds, ((0,), (0,)))

            @pl.when(t % 2 == 1)
            def _():
                sib_out[d] = acc[...].astype(BF16)
                sib_copy(d).start()

            @pl.when((t % 2 == 0) & (t > 0))
            def _():
                sib_copy(d).wait_recv()
                red_out[d] = (acc[...] + sib_in[d].astype(F32)).astype(BF16)
                for part in (0, 1):
                    red_copy(d, part, s).start()

        return 0

    lax.fori_loop(0, span, grad_step, 0)

    @pl.when(sibling > me)
    def _():
        sib_copy(0).wait_recv()
        acc[...] += sib_in[0].astype(F32)

    hd_out[0] = acc[1 - side].astype(BF16)
    swap = remote(hd_out.at[0], hd_in.at[0], hd_sem.at[0], hd_sem.at[1], twin)
    swap.start()

    for h in range(heads):
        dq_ref[:, h * HDIM:(h + 1) * HDIM] = (
            (dq_t[:, h * rows:(h + 1) * rows] * scaling).T.astype(BF16)
        )

    swap.wait()
    acc[side] += hd_in[0].astype(F32)

    for d, target in enumerate(partners, 1):
        @pl.when(target > me)
        def _():
            for source in (0, 1):
                red_arrival(d, source).wait_recv()
                acc[side] += red_in[d, source].astype(F32)

    hd_out[1] = (acc[side] * jnp.where(side == 0, scaling, 1.0)).astype(BF16)
    finished = remote(hd_out.at[1], hd_in.at[1], hd_sem.at[2], hd_sem.at[3], twin)
    finished.start()
    finished.wait()

    @pl.when(side == 0)
    def _():
        dk_ref[...] = hd_out[1]
        dv_ref[...] = hd_in[1]

    @pl.when(side != 0)
    def _():
        dk_ref[...] = hd_in[1]
        dv_ref[...] = hd_out[1]

    @pl.when(sibling > me)
    def _():
        own_copy(0, sibling).wait_send()

    @pl.when(sibling < me)
    def _():
        sib_copy(0).wait_send()

    for d, target in enumerate(partners, 1):
        @pl.when(target > me)
        def _():
            own_copy(d, target).wait_send()

        @pl.when(target < me)
        def _():
            relay_copy(d, target).wait_send()
            sib_copy(d).wait_send()
            for part in (0, 1):
                red_copy(d, part, target).wait_send()


def copy_out(a, b, c, out_a, out_b, out_c, sems):
    copies = [
        pltpu.make_async_copy(src, dst, sems.at[i])
        for i, (src, dst) in enumerate(((a, out_a), (b, out_b), (c, out_c)))
    ]
    for copy in copies:
        copy.start()
    for copy in copies:
        copy.wait()


def body(query, keys, values, grad_out, doc_start):
    rows = keys.shape[0]
    heads = query.shape[1] // HDIM
    wide = heads * rows
    span = MAXDOC // rows
    vmem = pl.BlockSpec(memory_space=pltpu.VMEM)
    pair = (2, rows, HDIM)
    grads = pl.pallas_call(
        functools.partial(kernel, span),
        out_shape=(
            jax.ShapeDtypeStruct(query.shape, BF16),
            jax.ShapeDtypeStruct(keys.shape, BF16),
            jax.ShapeDtypeStruct(values.shape, BF16),
        ),
        in_specs=[vmem] * 5,
        out_specs=(vmem,) * 3,
        scratch_shapes=[
            pltpu.VMEM((span,) + pair, BF16),
            pltpu.VMEM((wide, HDIM), BF16),
            pltpu.VMEM((wide, HDIM), BF16),
            pltpu.VMEM((HDIM, wide), BF16),
            pltpu.VMEM((HDIM, wide), BF16),
            pltpu.VMEM((span, rows, wide), F32),
            pltpu.VMEM((span, rows, wide), F32),
            pltpu.VMEM((span, 2, 1, wide), F32),
            pltpu.VMEM((1, wide), F32),
            pltpu.VMEM((1, wide), F32),
            pltpu.VMEM((1, wide), F32),
            pltpu.VMEM((HDIM, wide), F32),
            pltpu.VMEM(pair, F32),
            pltpu.VMEM((span // 2,) + pair, BF16),
            pltpu.VMEM((span // 2,) + pair, BF16),
            pltpu.VMEM((span // 2,) + pair, BF16),
            pltpu.VMEM((span // 2,) + pair, BF16),
            pltpu.VMEM(pair, BF16),
            pltpu.VMEM(pair, BF16),
            pltpu.SemaphoreType.DMA((span,)),
            pltpu.SemaphoreType.DMA((span,)),
            pltpu.SemaphoreType.DMA((span // 2,)),
            pltpu.SemaphoreType.DMA((span // 2,)),
            pltpu.SemaphoreType.DMA((span // 2, 2)),
            pltpu.SemaphoreType.DMA((span // 2, 2)),
            pltpu.SemaphoreType.DMA((4,)),
        ],
        compiler_params=pltpu.CompilerParams(
            collective_id=0, has_side_effects=True, vmem_limit_bytes=56 * 1024 * 1024
        ),
    )(query, keys, values, grad_out, doc_start.reshape(1, rows))
    anywhere = pl.BlockSpec(memory_space=pl.ANY)
    return pl.pallas_call(
        copy_out,
        out_shape=tuple(jax.ShapeDtypeStruct(g.shape, g.dtype) for g in grads),
        in_specs=[anywhere] * 3,
        out_specs=(anywhere,) * 3,
        scratch_shapes=[pltpu.SemaphoreType.DMA((3,))],
        compiler_params=pltpu.CompilerParams(vmem_limit_bytes=60 * 1024 * 1024),
    )(*grads)


def solution(mesh):
    in_specs = (P("cp", "hd"), P("cp", None), P("cp", None), P("cp", "hd"), P("cp"))
    out_specs = (P("cp", "hd"), P("cp", None), P("cp", None))
    return jax.shard_map(body, mesh=mesh, in_specs=in_specs, out_specs=out_specs, check_vma=False)
```

```python
import functools
import math

import jax
import jax.numpy as jnp
from jax import lax
from jax.experimental import pallas as pl
from jax.experimental.pallas import tpu as pltpu
from jax.sharding import PartitionSpec as P

HDIM = 128
MAXDOC = 4096
MESH = pl.DeviceIdType.MESH
BF16 = jnp.bfloat16
F32 = jnp.float32
MASKED = -1e30


def xor3(a, b):
    out = 0
    for bit in (1, 2, 4):
        x, y = (a // bit) % 2, (b // bit) % 2
        out = out + bit * (x + y - 2 * x * y)
    return out


def dot(a, b, contract=((1,), (0,))):
    return lax.dot_general(a, b, (contract, ((), ())), preferred_element_type=F32)


def kernel(
    span,
    q_ref, k_ref, v_ref, do_ref, start_ref,
    dq_ref, dk_ref, dv_ref,
    kv, qs, dos, qt, dot_t, e_all, d_all, raw0, raw1, p0, p1, ds0, ds1, m_run, l_run, w_run, dq_t, acc,
    sib_out, sib_in, red_out, red_in, hd_out, hd_in,
    kv_send, kv_recv, sib_send, sib_recv, red_send, red_recv, hd_sem,
):
    rows = k_ref.shape[0]
    heads = q_ref.shape[1] // HDIM
    wide = heads * rows
    chunk = rows // 2
    tile = rows // 2
    piece = 32
    raw, p_halves, ds_halves = (raw0, raw1), (p0, p1), (ds0, ds1)
    scaling = 1.0 / math.sqrt(HDIM)
    scale2 = scaling * math.log2(math.e)

    pos = lax.axis_index("cp")
    me = pos % span
    base = pos - me
    side = lax.axis_index("hd")
    twin = {"hd": 1 - side}

    def peer(index, hd=None):
        return {"cp": base + index} if hd is None else {"cp": base + index, "hd": hd}

    sibling = xor3(me, 1)
    partners = [xor3(me, 2 * d) for d in range(1, span // 2)]

    barrier = pltpu.get_barrier_semaphore()
    for other in [peer(sibling), twin] + [peer(p, hd) for p in partners for hd in (0, 1)]:
        pl.semaphore_signal(barrier, inc=1, device_id=other, device_id_type=MESH)
    pl.semaphore_wait(barrier, 2 + 2 * len(partners))

    def remote(src, dst, send, recv, device):
        return pltpu.make_async_remote_copy(
            src_ref=src, dst_ref=dst, send_sem=send, recv_sem=recv,
            device_id=device, device_id_type=MESH,
        )

    def own_copy(d, target):
        return remote(kv.at[me], kv.at[me], kv_send.at[d], kv_recv.at[me], peer(target))

    def relay_copy(d, slot):
        return remote(
            kv.at[slot], kv.at[slot], kv_send.at[span // 2 + d], kv_recv.at[slot], peer(sibling)
        )

    def sib_copy(d):
        return remote(
            sib_out.at[d], sib_in.at[d], sib_send.at[d], sib_recv.at[d], peer(sibling)
        )

    def red_copy(d, part, target):
        return remote(
            red_out.at[d, part], red_in.at[d, side], red_send.at[d, part],
            red_recv.at[d, side], peer(target, part),
        )

    def red_arrival(d, source):
        return remote(
            red_out.at[d, 0], red_in.at[d, source], red_send.at[d, 0],
            red_recv.at[d, source], twin,
        )

    kv[me, 0] = k_ref[...]
    kv[me, 1] = v_ref[...]
    for d, target in enumerate(partners, 1):
        @pl.when(target > me)
        def _():
            own_copy(d, target).start()

    @pl.when(sibling > me)
    def _():
        own_copy(0, sibling).start()

    for h in range(heads):
        at = slice(h * rows, (h + 1) * rows)
        q = q_ref[:, h * HDIM:(h + 1) * HDIM]
        g = do_ref[:, h * HDIM:(h + 1) * HDIM]
        qs[at, :] = q
        dos[at, :] = g
        qt[:, at] = q.T
        dot_t[:, at] = g.T
    m_run[...] = jnp.full_like(m_run, MASKED)
    l_run[...] = jnp.zeros_like(l_run)
    w_run[...] = jnp.zeros_like(w_run)
    dq_t[...] = jnp.zeros_like(dq_t)

    def load_tile(s, tq):
        at_q = slice(tq * tile, (tq + 1) * tile)
        raw[tq % 2][...] = dot(kv[s, 0], qt[:, at_q])
        d_all[s, :, at_q] = dot(kv[s, 1], dot_t[:, at_q])

    def stat_tile(s, tq, diagonal):
        at_q = slice(tq * tile, (tq + 1) * tile)
        row0 = (tq * tile) % rows
        source = raw[tq % 2]
        first = start_ref[:, row0:row0 + tile] - (base + s) * rows
        key_pos = lax.broadcasted_iota(jnp.int32, (piece, tile), 0)
        if diagonal:
            query_pos = lax.broadcasted_iota(jnp.int32, (piece, tile), 1) + row0
        old = m_run[:, at_q]
        top = jnp.broadcast_to(old, (8, tile))
        for r in range(0, rows, piece):
            at_k = slice(r, r + piece)
            allowed = key_pos >= first - r
            if diagonal:
                allowed = allowed & (key_pos + r <= query_pos)
            scores = jnp.where(allowed, source[at_k, :] * scale2, MASKED)
            e_all[s, at_k, at_q] = scores
            top = jnp.maximum(top, jnp.max(scores.reshape(piece // 8, 8, tile), axis=0))
        new = jnp.max(top, axis=0, keepdims=True)
        total = jnp.zeros((8, tile), F32)
        weighted = jnp.zeros((8, tile), F32)
        for r in range(0, rows, piece):
            at_k = slice(r, r + piece)
            e = jnp.exp2(e_all[s, at_k, at_q] - new)
            ed = e * d_all[s, at_k, at_q]
            total = total + jnp.sum(e.reshape(piece // 8, 8, tile), axis=0)
            weighted = weighted + jnp.sum(ed.reshape(piece // 8, 8, tile), axis=0)
        fac = jnp.exp2(old - new)
        l_run[:, at_q] = l_run[:, at_q] * fac + jnp.sum(total, axis=0, keepdims=True)
        w_run[:, at_q] = w_run[:, at_q] * fac + jnp.sum(weighted, axis=0, keepdims=True)
        m_run[:, at_q] = new

    def stat_block(s, diagonal):
        load_tile(s, 0)
        for tq in range(wide // tile):
            if tq + 1 < wide // tile:
                load_tile(s, tq + 1)
            stat_tile(s, tq, diagonal)

    stat_block(me, True)

    def stat_step(t, _):
        s = xor3(me, t)

        @pl.when(s < me)
        def _():
            relay_copy(0, s).wait_recv()

            @pl.when(t % 2 == 0)
            def _():
                relay_copy(t // 2, s).start()

            stat_block(s, False)

        return 0

    lax.fori_loop(1, span, stat_step, 0)

    w_run[...] = w_run[...] / l_run[...]
    m_run[...] = m_run[...] + jnp.log2(l_run[...])

    def grad_step(i, _):
        t = span - 1 - i
        s = xor3(me, t)
        d = t // 2

        @pl.when(s <= me)
        def _():
            dq_term = None
            for kc in range(rows // chunk):
                p_low, ds_low = p_halves[kc], ds_halves[kc]
                for tq in range(wide // tile):
                    at_q = slice(tq * tile, (tq + 1) * tile)
                    norm, delta = m_run[:, at_q], w_run[:, at_q]
                    for r in range(0, chunk, piece):
                        at_k = slice(kc * chunk + r, kc * chunk + r + piece)
                        p = jnp.exp2(e_all[s, at_k, at_q] - norm)
                        ds = p * (d_all[s, at_k, at_q] - delta)
                        p_low[r:r + piece, at_q] = p.astype(BF16)
                        ds_low[r:r + piece, at_q] = ds.astype(BF16)
                at_k = slice(kc * chunk, (kc + 1) * chunk)
                acc[0, at_k, :] = dot(ds_low[...], qs[...])
                acc[1, at_k, :] = dot(p_low[...], dos[...])
                term = dot(kv[s, 0, at_k, :], ds_low[...], ((0,), (0,)))
                dq_term = term if dq_term is None else dq_term + term
            dq_t[...] += dq_term

            @pl.when(t % 2 == 1)
            def _():
                sib_out[d] = acc[...].astype(BF16)
                sib_copy(d).start()

            @pl.when((t % 2 == 0) & (t > 0))
            def _():
                sib_copy(d).wait_recv()
                red_out[d] = (acc[...] + sib_in[d].astype(F32)).astype(BF16)
                for part in (0, 1):
                    red_copy(d, part, s).start()

        return 0

    lax.fori_loop(0, span, grad_step, 0)

    @pl.when(sibling > me)
    def _():
        sib_copy(0).wait_recv()
        acc[...] += sib_in[0].astype(F32)

    hd_out[0] = acc[1 - side].astype(BF16)
    swap = remote(hd_out.at[0], hd_in.at[0], hd_sem.at[0], hd_sem.at[1], twin)
    swap.start()

    for h in range(heads):
        dq_ref[:, h * HDIM:(h + 1) * HDIM] = (
            (dq_t[:, h * rows:(h + 1) * rows] * scaling).T.astype(BF16)
        )

    swap.wait()
    acc[side] += hd_in[0].astype(F32)

    for d, target in enumerate(partners, 1):
        @pl.when(target > me)
        def _():
            for source in (0, 1):
                red_arrival(d, source).wait_recv()
                acc[side] += red_in[d, source].astype(F32)

    hd_out[1] = (acc[side] * jnp.where(side == 0, scaling, 1.0)).astype(BF16)
    finished = remote(hd_out.at[1], hd_in.at[1], hd_sem.at[2], hd_sem.at[3], twin)
    finished.start()
    finished.wait()

    @pl.when(side == 0)
    def _():
        dk_ref[...] = hd_out[1]
        dv_ref[...] = hd_in[1]

    @pl.when(side != 0)
    def _():
        dk_ref[...] = hd_in[1]
        dv_ref[...] = hd_out[1]

    @pl.when(sibling > me)
    def _():
        own_copy(0, sibling).wait_send()

    @pl.when(sibling < me)
    def _():
        sib_copy(0).wait_send()

    for d, target in enumerate(partners, 1):
        @pl.when(target > me)
        def _():
            own_copy(d, target).wait_send()

        @pl.when(target < me)
        def _():
            relay_copy(d, target).wait_send()
            sib_copy(d).wait_send()
            for part in (0, 1):
                red_copy(d, part, target).wait_send()


def copy_out(a, b, c, out_a, out_b, out_c):
    out_a[...] = a[...]
    out_b[...] = b[...]
    out_c[...] = c[...]


def body(query, keys, values, grad_out, doc_start):
    rows = keys.shape[0]
    heads = query.shape[1] // HDIM
    wide = heads * rows
    span = MAXDOC // rows
    vmem = pl.BlockSpec(memory_space=pltpu.VMEM)
    pair = (2, rows, HDIM)
    grads = pl.pallas_call(
        functools.partial(kernel, span),
        out_shape=(
            jax.ShapeDtypeStruct(query.shape, BF16),
            jax.ShapeDtypeStruct(keys.shape, BF16),
            jax.ShapeDtypeStruct(values.shape, BF16),
        ),
        in_specs=[vmem] * 5,
        out_specs=(vmem,) * 3,
        scratch_shapes=[
            pltpu.VMEM((span,) + pair, BF16),
            pltpu.VMEM((wide, HDIM), BF16),
            pltpu.VMEM((wide, HDIM), BF16),
            pltpu.VMEM((HDIM, wide), BF16),
            pltpu.VMEM((HDIM, wide), BF16),
            pltpu.VMEM((span, rows, wide), F32),
            pltpu.VMEM((span, rows, wide), F32),
            pltpu.VMEM((rows, rows // 2), F32),
            pltpu.VMEM((rows, rows // 2), F32),
            pltpu.VMEM((rows // 2, wide), BF16),
            pltpu.VMEM((rows // 2, wide), BF16),
            pltpu.VMEM((rows // 2, wide), BF16),
            pltpu.VMEM((rows // 2, wide), BF16),
            pltpu.VMEM((1, wide), F32),
            pltpu.VMEM((1, wide), F32),
            pltpu.VMEM((1, wide), F32),
            pltpu.VMEM((HDIM, wide), F32),
            pltpu.VMEM(pair, F32),
            pltpu.VMEM((span // 2,) + pair, BF16),
            pltpu.VMEM((span // 2,) + pair, BF16),
            pltpu.VMEM((span // 2,) + pair, BF16),
            pltpu.VMEM((span // 2,) + pair, BF16),
            pltpu.VMEM(pair, BF16),
            pltpu.VMEM(pair, BF16),
            pltpu.SemaphoreType.DMA((span,)),
            pltpu.SemaphoreType.DMA((span,)),
            pltpu.SemaphoreType.DMA((span // 2,)),
            pltpu.SemaphoreType.DMA((span // 2,)),
            pltpu.SemaphoreType.DMA((span // 2, 2)),
            pltpu.SemaphoreType.DMA((span // 2, 2)),
            pltpu.SemaphoreType.DMA((4,)),
        ],
        compiler_params=pltpu.CompilerParams(
            collective_id=0, has_side_effects=True, vmem_limit_bytes=56 * 1024 * 1024
        ),
    )(query, keys, values, grad_out, doc_start.reshape(1, rows))
    return pl.pallas_call(
        copy_out,
        out_shape=tuple(jax.ShapeDtypeStruct(g.shape, g.dtype) for g in grads),
        in_specs=[vmem] * 3,
        out_specs=(vmem,) * 3,
        compiler_params=pltpu.CompilerParams(vmem_limit_bytes=60 * 1024 * 1024),
    )(*grads)


def solution(mesh):
    in_specs = (P("cp", "hd"), P("cp", None), P("cp", None), P("cp", "hd"), P("cp"))
    out_specs = (P("cp", "hd"), P("cp", None), P("cp", None))
    return jax.shard_map(body, mesh=mesh, in_specs=in_specs, out_specs=out_specs, check_vma=False)
```

```python
import functools
import math

import jax
import jax.numpy as jnp
from jax import lax
from jax.experimental import pallas as pl
from jax.experimental.pallas import tpu as pltpu
from jax.sharding import PartitionSpec as P

HDIM = 128
MAXDOC = 4096
MESH = pl.DeviceIdType.MESH
BF16 = jnp.bfloat16
F32 = jnp.float32
MASKED = -1e30


def xor3(a, b):
    out = 0
    for bit in (1, 2, 4):
        x, y = (a // bit) % 2, (b // bit) % 2
        out = out + bit * (x + y - 2 * x * y)
    return out


def dot(a, b, contract=((1,), (0,))):
    return lax.dot_general(a, b, (contract, ((), ())), preferred_element_type=F32)


def kernel(
    span,
    q_ref, k_ref, v_ref, do_ref, start_ref,
    dq_ref, dk_ref, dv_ref,
    kv, qs, dos, qt, dot_t, e_all, d_all, raw0, raw1, p0, p1, ds0, ds1, m_run, l_run, w_run, dq_t, acc,
    sib_out, sib_in, red_out, red_in, hd_out, hd_in,
    kv_send, kv_recv, sib_send, sib_recv, red_send, red_recv, hd_sem,
):
    rows = k_ref.shape[0]
    heads = q_ref.shape[1] // HDIM
    wide = heads * rows
    chunk = rows // 2
    tile = rows // 2
    piece = 32
    raw, p_halves, ds_halves = (raw0, raw1), (p0, p1), (ds0, ds1)
    scaling = 1.0 / math.sqrt(HDIM)
    scale2 = scaling * math.log2(math.e)

    pos = lax.axis_index("cp")
    me = pos % span
    base = pos - me
    side = lax.axis_index("hd")
    twin = {"hd": 1 - side}

    def peer(index, hd=None):
        return {"cp": base + index} if hd is None else {"cp": base + index, "hd": hd}

    sibling = xor3(me, 1)
    partners = [xor3(me, 2 * d) for d in range(1, span // 2)]

    barrier = pltpu.get_barrier_semaphore()
    for other in [peer(sibling), twin] + [peer(p, hd) for p in partners for hd in (0, 1)]:
        pl.semaphore_signal(barrier, inc=1, device_id=other, device_id_type=MESH)
    pl.semaphore_wait(barrier, 2 + 2 * len(partners))

    def remote(src, dst, send, recv, device):
        return pltpu.make_async_remote_copy(
            src_ref=src, dst_ref=dst, send_sem=send, recv_sem=recv,
            device_id=device, device_id_type=MESH,
        )

    def kv_copy(slot, part, send, device):
        return remote(
            kv.at[slot, part], kv.at[slot, part], kv_send.at[send, part],
            kv_recv.at[slot, part], device,
        )

    def own_parts(d):
        return (0, 1) if d <= 1 else (side,)

    def sib_copy(d):
        return remote(
            sib_out.at[d], sib_in.at[d], sib_send.at[d], sib_recv.at[d], peer(sibling)
        )

    def red_copy(d, part, target):
        return remote(
            red_out.at[d, part], red_in.at[d, side], red_send.at[d, part],
            red_recv.at[d, side], peer(target, part),
        )

    def red_arrival(d, source):
        return remote(
            red_out.at[d, 0], red_in.at[d, source], red_send.at[d, 0],
            red_recv.at[d, source], twin,
        )

    kv[me, 0] = k_ref[...]
    kv[me, 1] = v_ref[...]
    for d, target in enumerate(partners, 1):
        @pl.when(target > me)
        def _():
            for part in own_parts(d):
                kv_copy(me, part, d, peer(target)).start()

    @pl.when(sibling > me)
    def _():
        for part in (0, 1):
            kv_copy(me, part, 0, peer(sibling)).start()

    for h in range(heads):
        at = slice(h * rows, (h + 1) * rows)
        q = q_ref[:, h * HDIM:(h + 1) * HDIM]
        g = do_ref[:, h * HDIM:(h + 1) * HDIM]
        qs[at, :] = q
        dos[at, :] = g
        qt[:, at] = q.T
        dot_t[:, at] = g.T
    m_run[...] = jnp.full_like(m_run, MASKED)
    l_run[...] = jnp.zeros_like(l_run)
    w_run[...] = jnp.zeros_like(w_run)
    dq_t[...] = jnp.zeros_like(dq_t)

    def load_tile(s, tq):
        at_q = slice(tq * tile, (tq + 1) * tile)
        raw[tq % 2][...] = dot(kv[s, 0], qt[:, at_q])
        d_all[s, :, at_q] = dot(kv[s, 1], dot_t[:, at_q])

    def stat_tile(s, tq, diagonal):
        at_q = slice(tq * tile, (tq + 1) * tile)
        row0 = (tq * tile) % rows
        source = raw[tq % 2]
        first = start_ref[:, row0:row0 + tile] - (base + s) * rows
        key_pos = lax.broadcasted_iota(jnp.int32, (piece, tile), 0)
        if diagonal:
            query_pos = lax.broadcasted_iota(jnp.int32, (piece, tile), 1) + row0
        old = m_run[:, at_q]
        top = jnp.broadcast_to(old, (8, tile))
        for r in range(0, rows, piece):
            at_k = slice(r, r + piece)
            allowed = key_pos >= first - r
            if diagonal:
                allowed = allowed & (key_pos + r <= query_pos)
            scores = jnp.where(allowed, source[at_k, :] * scale2, MASKED)
            e_all[s, at_k, at_q] = scores
            top = jnp.maximum(top, jnp.max(scores.reshape(piece // 8, 8, tile), axis=0))
        new = jnp.max(top, axis=0, keepdims=True)
        total = jnp.zeros((8, tile), F32)
        weighted = jnp.zeros((8, tile), F32)
        for r in range(0, rows, piece):
            at_k = slice(r, r + piece)
            e = jnp.exp2(e_all[s, at_k, at_q] - new)
            ed = e * d_all[s, at_k, at_q]
            total = total + jnp.sum(e.reshape(piece // 8, 8, tile), axis=0)
            weighted = weighted + jnp.sum(ed.reshape(piece // 8, 8, tile), axis=0)
        fac = jnp.exp2(old - new)
        l_run[:, at_q] = l_run[:, at_q] * fac + jnp.sum(total, axis=0, keepdims=True)
        w_run[:, at_q] = w_run[:, at_q] * fac + jnp.sum(weighted, axis=0, keepdims=True)
        m_run[:, at_q] = new

    def stat_block(s, diagonal):
        load_tile(s, 0)
        for tq in range(wide // tile):
            if tq + 1 < wide // tile:
                load_tile(s, tq + 1)
            stat_tile(s, tq, diagonal)

    stat_block(me, True)

    def stat_step(t, _):
        s = xor3(me, t)

        @pl.when(s < me)
        def _():
            d = t // 2

            @pl.when(t >= 4)
            def _():
                @pl.when(t % 2 == 0)
                def _():
                    kv_copy(s, side, 0, twin).wait_recv()
                    kv_copy(s, side, span + d, twin).start()
                    kv_copy(s, side, span // 2 + d, peer(sibling)).start()
                    kv_copy(s, 1 - side, 0, twin).wait_recv()
                    kv_copy(s, 1 - side, span // 2 + d, peer(sibling)).start()

                @pl.when(t % 2 == 1)
                def _():
                    for part in (0, 1):
                        kv_copy(s, part, 0, twin).wait_recv()

            @pl.when(t < 4)
            def _():
                for part in (0, 1):
                    kv_copy(s, part, 0, twin).wait_recv()

                @pl.when(t == 2)
                def _():
                    for part in (0, 1):
                        kv_copy(s, part, span // 2 + d, peer(sibling)).start()

            stat_block(s, False)

        return 0

    lax.fori_loop(1, span, stat_step, 0)

    w_run[...] = w_run[...] / l_run[...]
    m_run[...] = m_run[...] + jnp.log2(l_run[...])

    def grad_step(i, _):
        t = span - 1 - i
        s = xor3(me, t)
        d = t // 2

        @pl.when(s <= me)
        def _():
            dq_term = None
            for kc in range(rows // chunk):
                p_low, ds_low = p_halves[kc], ds_halves[kc]
                for tq in range(wide // tile):
                    at_q = slice(tq * tile, (tq + 1) * tile)
                    norm, delta = m_run[:, at_q], w_run[:, at_q]
                    for r in range(0, chunk, piece):
                        at_k = slice(kc * chunk + r, kc * chunk + r + piece)
                        p = jnp.exp2(e_all[s, at_k, at_q] - norm)
                        ds = p * (d_all[s, at_k, at_q] - delta)
                        p_low[r:r + piece, at_q] = p.astype(BF16)
                        ds_low[r:r + piece, at_q] = ds.astype(BF16)
                at_k = slice(kc * chunk, (kc + 1) * chunk)
                acc[0, at_k, :] = dot(ds_low[...], qs[...])
                acc[1, at_k, :] = dot(p_low[...], dos[...])
                term = dot(kv[s, 0, at_k, :], ds_low[...], ((0,), (0,)))
                dq_term = term if dq_term is None else dq_term + term
            dq_t[...] += dq_term

            @pl.when(t % 2 == 1)
            def _():
                sib_out[d] = acc[...].astype(BF16)
                sib_copy(d).start()

            @pl.when((t % 2 == 0) & (t > 0))
            def _():
                sib_copy(d).wait_recv()
                red_out[d] = (acc[...] + sib_in[d].astype(F32)).astype(BF16)
                for part in (0, 1):
                    red_copy(d, part, s).start()

        return 0

    lax.fori_loop(0, span, grad_step, 0)

    @pl.when(sibling > me)
    def _():
        sib_copy(0).wait_recv()
        acc[...] += sib_in[0].astype(F32)

    hd_out[0] = acc[1 - side].astype(BF16)
    swap = remote(hd_out.at[0], hd_in.at[0], hd_sem.at[0], hd_sem.at[1], twin)
    swap.start()

    for h in range(heads):
        dq_ref[:, h * HDIM:(h + 1) * HDIM] = (
            (dq_t[:, h * rows:(h + 1) * rows] * scaling).T.astype(BF16)
        )

    swap.wait()
    acc[side] += hd_in[0].astype(F32)

    for d, target in enumerate(partners, 1):
        @pl.when(target > me)
        def _():
            for source in (0, 1):
                red_arrival(d, source).wait_recv()
                acc[side] += red_in[d, source].astype(F32)

    hd_out[1] = (acc[side] * jnp.where(side == 0, scaling, 1.0)).astype(BF16)
    finished = remote(hd_out.at[1], hd_in.at[1], hd_sem.at[2], hd_sem.at[3], twin)
    finished.start()
    finished.wait()

    @pl.when(side == 0)
    def _():
        dk_ref[...] = hd_out[1]
        dv_ref[...] = hd_in[1]

    @pl.when(side != 0)
    def _():
        dk_ref[...] = hd_in[1]
        dv_ref[...] = hd_out[1]

    @pl.when(sibling > me)
    def _():
        for part in (0, 1):
            kv_copy(me, part, 0, peer(sibling)).wait_send()

    @pl.when(sibling < me)
    def _():
        sib_copy(0).wait_send()

    for d, target in enumerate(partners, 1):
        @pl.when(target > me)
        def _():
            for part in own_parts(d):
                kv_copy(me, part, d, peer(target)).wait_send()

        @pl.when(target < me)
        def _():
            for part in (0, 1):
                kv_copy(target, part, span // 2 + d, peer(sibling)).wait_send()
            if d > 1:
                kv_copy(target, side, span + d, twin).wait_send()
            sib_copy(d).wait_send()
            for part in (0, 1):
                red_copy(d, part, target).wait_send()


def copy_out(a, b, c, out_a, out_b, out_c):
    out_a[...] = a[...]
    out_b[...] = b[...]
    out_c[...] = c[...]


def body(query, keys, values, grad_out, doc_start):
    rows = keys.shape[0]
    heads = query.shape[1] // HDIM
    wide = heads * rows
    span = MAXDOC // rows
    vmem = pl.BlockSpec(memory_space=pltpu.VMEM)
    pair = (2, rows, HDIM)
    grads = pl.pallas_call(
        functools.partial(kernel, span),
        out_shape=(
            jax.ShapeDtypeStruct(query.shape, BF16),
            jax.ShapeDtypeStruct(keys.shape, BF16),
            jax.ShapeDtypeStruct(values.shape, BF16),
        ),
        in_specs=[vmem] * 5,
        out_specs=(vmem,) * 3,
        scratch_shapes=[
            pltpu.VMEM((span,) + pair, BF16),
            pltpu.VMEM((wide, HDIM), BF16),
            pltpu.VMEM((wide, HDIM), BF16),
            pltpu.VMEM((HDIM, wide), BF16),
            pltpu.VMEM((HDIM, wide), BF16),
            pltpu.VMEM((span, rows, wide), F32),
            pltpu.VMEM((span, rows, wide), F32),
            pltpu.VMEM((rows, rows // 2), F32),
            pltpu.VMEM((rows, rows // 2), F32),
            pltpu.VMEM((rows // 2, wide), BF16),
            pltpu.VMEM((rows // 2, wide), BF16),
            pltpu.VMEM((rows // 2, wide), BF16),
            pltpu.VMEM((rows // 2, wide), BF16),
            pltpu.VMEM((1, wide), F32),
            pltpu.VMEM((1, wide), F32),
            pltpu.VMEM((1, wide), F32),
            pltpu.VMEM((HDIM, wide), F32),
            pltpu.VMEM(pair, F32),
            pltpu.VMEM((span // 2,) + pair, BF16),
            pltpu.VMEM((span // 2,) + pair, BF16),
            pltpu.VMEM((span // 2,) + pair, BF16),
            pltpu.VMEM((span // 2,) + pair, BF16),
            pltpu.VMEM(pair, BF16),
            pltpu.VMEM(pair, BF16),
            pltpu.SemaphoreType.DMA((2 * span, 2)),
            pltpu.SemaphoreType.DMA((span, 2)),
            pltpu.SemaphoreType.DMA((span // 2,)),
            pltpu.SemaphoreType.DMA((span // 2,)),
            pltpu.SemaphoreType.DMA((span // 2, 2)),
            pltpu.SemaphoreType.DMA((span // 2, 2)),
            pltpu.SemaphoreType.DMA((4,)),
        ],
        compiler_params=pltpu.CompilerParams(
            collective_id=0, has_side_effects=True, vmem_limit_bytes=56 * 1024 * 1024
        ),
    )(query, keys, values, grad_out, doc_start.reshape(1, rows))
    return pl.pallas_call(
        copy_out,
        out_shape=tuple(jax.ShapeDtypeStruct(g.shape, g.dtype) for g in grads),
        in_specs=[vmem] * 3,
        out_specs=(vmem,) * 3,
        compiler_params=pltpu.CompilerParams(vmem_limit_bytes=60 * 1024 * 1024),
    )(*grads)


def solution(mesh):
    in_specs = (P("cp", "hd"), P("cp", None), P("cp", None), P("cp", "hd"), P("cp"))
    out_specs = (P("cp", "hd"), P("cp", None), P("cp", None))
    return jax.shard_map(body, mesh=mesh, in_specs=in_specs, out_specs=out_specs, check_vma=False)
```

```python
import functools
import math

import jax
import jax.numpy as jnp
from jax import lax
from jax.experimental import pallas as pl
from jax.experimental.pallas import tpu as pltpu
from jax.sharding import PartitionSpec as P

HDIM = 128
MAXDOC = 4096
MESH = pl.DeviceIdType.MESH
BF16 = jnp.bfloat16
F32 = jnp.float32
MASKED = -1e30


def xor3(a, b):
    out = 0
    for bit in (1, 2, 4):
        x, y = (a // bit) % 2, (b // bit) % 2
        out = out + bit * (x + y - 2 * x * y)
    return out


def dot(a, b, contract=((1,), (0,))):
    return lax.dot_general(a, b, (contract, ((), ())), preferred_element_type=F32)


def kernel(
    span,
    q_ref, k_ref, v_ref, do_ref, start_ref,
    dq_ref, dk_ref, dv_ref,
    kv, qs, dos, qt, dot_t, e_all, d_all, raw0, raw1, p0, p1, ds0, ds1, m_run, l_run, w_run, dq_t, acc, own,
    sib_out, sib_in, red_out, red_in, hd_out, hd_in,
    far_q, far_do, far_stat, stat_out, far_dq, far_dq_out, far_dq_in, mid_out, mid_in,
    kv_send, kv_recv, sib_send, sib_recv, red_send, red_recv, hd_sem, far_send, far_recv,
):
    rows = k_ref.shape[0]
    heads = q_ref.shape[1] // HDIM
    wide = heads * rows
    chunk = rows // 2
    tile = rows // 2
    piece = 32
    raw, p_halves, ds_halves = (raw0, raw1), (p0, p1), (ds0, ds1)
    scaling = 1.0 / math.sqrt(HDIM)
    scale2 = scaling * math.log2(math.e)

    pos = lax.axis_index("cp")
    me = pos % span
    base = pos - me
    side = lax.axis_index("hd")
    twin = {"hd": 1 - side}

    def peer(index, hd=None):
        return {"cp": base + index} if hd is None else {"cp": base + index, "hd": hd}

    sibling = xor3(me, 1)
    partners = [xor3(me, 2 * d) for d in range(1, span // 2)]

    barrier = pltpu.get_barrier_semaphore()
    greeted = [peer(sibling), twin, peer(partners[2])]
    greeted += [peer(p, hd) for p in partners[:2] for hd in (0, 1)]
    for other in greeted:
        pl.semaphore_signal(barrier, inc=1, device_id=other, device_id_type=MESH)
    pl.semaphore_wait(barrier, len(greeted))

    def remote(src, dst, send, recv, device):
        return pltpu.make_async_remote_copy(
            src_ref=src, dst_ref=dst, send_sem=send, recv_sem=recv,
            device_id=device, device_id_type=MESH,
        )

    def own_copy(d, target):
        return remote(kv.at[me], kv.at[me], kv_send.at[d], kv_recv.at[me], peer(target))

    def relay_copy(d, slot):
        return remote(
            kv.at[slot], kv.at[slot], kv_send.at[span // 2 + d], kv_recv.at[slot], peer(sibling)
        )

    def sib_copy(d):
        return remote(
            sib_out.at[d], sib_in.at[d], sib_send.at[d], sib_recv.at[d], peer(sibling)
        )

    def red_copy(d, part, target):
        return remote(
            red_out.at[d, part], red_in.at[d, side], red_send.at[d, part],
            red_recv.at[d, side], peer(target, part),
        )

    helps, relays, owns = me // 2 == 1, me // 2 == 2, me // 2 == 3
    across = peer(partners[1])

    def far_copy(i):
        src, dst = (
            (qs, far_q), (dos, far_do), (stat_out, far_stat), (far_dq_out, far_dq_in),
        )[i]
        return remote(src, dst, far_send.at[i], far_recv.at[i], across)

    mid_copy = remote(mid_out, mid_in, far_send.at[4], far_recv.at[4], peer(partners[0]))

    def red_arrival(d, source):
        return remote(
            red_out.at[d, 0], red_in.at[d, source], red_send.at[d, 0],
            red_recv.at[d, source], twin,
        )

    kv[me, 0] = k_ref[...]
    kv[me, 1] = v_ref[...]
    for d, target in enumerate(partners, 1):
        @pl.when(target > me)
        def _():
            own_copy(d, target).start()

    @pl.when(sibling > me)
    def _():
        own_copy(0, sibling).start()

    for h in range(heads):
        at = slice(h * rows, (h + 1) * rows)
        q = q_ref[:, h * HDIM:(h + 1) * HDIM]
        g = do_ref[:, h * HDIM:(h + 1) * HDIM]
        qs[at, :] = q
        dos[at, :] = g
        qt[:, at] = q.T
        dot_t[:, at] = g.T

    @pl.when(owns)
    def _():
        far_copy(0).start()
        far_copy(1).start()

    m_run[...] = jnp.full_like(m_run, MASKED)
    l_run[...] = jnp.zeros_like(l_run)
    w_run[...] = jnp.zeros_like(w_run)
    dq_t[...] = jnp.zeros_like(dq_t)

    def load_tile(s, tq):
        at_q = slice(tq * tile, (tq + 1) * tile)
        raw[tq % 2][...] = dot(kv[s, 0], qt[:, at_q])
        d_all[s, :, at_q] = dot(kv[s, 1], dot_t[:, at_q])

    def stat_tile(s, tq, diagonal):
        at_q = slice(tq * tile, (tq + 1) * tile)
        row0 = (tq * tile) % rows
        source = raw[tq % 2]
        first = start_ref[:, row0:row0 + tile] - (base + s) * rows
        key_pos = lax.broadcasted_iota(jnp.int32, (piece, tile), 0)
        if diagonal:
            query_pos = lax.broadcasted_iota(jnp.int32, (piece, tile), 1) + row0
        old = m_run[:, at_q]
        top = jnp.broadcast_to(old, (8, tile))
        for r in range(0, rows, piece):
            at_k = slice(r, r + piece)
            allowed = key_pos >= first - r
            if diagonal:
                allowed = allowed & (key_pos + r <= query_pos)
            scores = jnp.where(allowed, source[at_k, :] * scale2, MASKED)
            e_all[s, at_k, at_q] = scores
            top = jnp.maximum(top, jnp.max(scores.reshape(piece // 8, 8, tile), axis=0))
        new = jnp.max(top, axis=0, keepdims=True)
        total = jnp.zeros((8, tile), F32)
        weighted = jnp.zeros((8, tile), F32)
        for r in range(0, rows, piece):
            at_k = slice(r, r + piece)
            e = jnp.exp2(e_all[s, at_k, at_q] - new)
            ed = e * d_all[s, at_k, at_q]
            total = total + jnp.sum(e.reshape(piece // 8, 8, tile), axis=0)
            weighted = weighted + jnp.sum(ed.reshape(piece // 8, 8, tile), axis=0)
        fac = jnp.exp2(old - new)
        l_run[:, at_q] = l_run[:, at_q] * fac + jnp.sum(total, axis=0, keepdims=True)
        w_run[:, at_q] = w_run[:, at_q] * fac + jnp.sum(weighted, axis=0, keepdims=True)
        m_run[:, at_q] = new

    def stat_block(s, diagonal):
        load_tile(s, 0)
        for tq in range(wide // tile):
            if tq + 1 < wide // tile:
                load_tile(s, tq + 1)
            stat_tile(s, tq, diagonal)

    stat_block(me, True)

    def stat_step(t, _):
        s = xor3(me, t)

        @pl.when(s < me)
        def _():
            relay_copy(0, s).wait_recv()

            @pl.when(t % 2 == 0)
            def _():
                relay_copy(t // 2, s).start()

            stat_block(s, False)

        return 0

    lax.fori_loop(1, span, stat_step, 0)

    w_run[...] = w_run[...] / l_run[...]
    m_run[...] = m_run[...] + jnp.log2(l_run[...])

    @pl.when(owns)
    def _():
        stat_out[0] = m_run[...]
        stat_out[1] = w_run[...]
        for h in range(heads):
            stat_out[2, :, h * rows:(h + 1) * rows] = start_ref[...].astype(F32)
        far_copy(2).start()

    def grad_block(slot, s, norm_of, delta_of, q_rows, do_rows, dq_sum, add):
        dq_term = None
        for kc in range(rows // chunk):
            p_low, ds_low = p_halves[kc], ds_halves[kc]
            for tq in range(wide // tile):
                at_q = slice(tq * tile, (tq + 1) * tile)
                norm, delta = norm_of(at_q), delta_of(at_q)
                for r in range(0, chunk, piece):
                    at_k = slice(kc * chunk + r, kc * chunk + r + piece)
                    p = jnp.exp2(e_all[slot, at_k, at_q] - norm)
                    ds = p * (d_all[slot, at_k, at_q] - delta)
                    p_low[r:r + piece, at_q] = p.astype(BF16)
                    ds_low[r:r + piece, at_q] = ds.astype(BF16)
            at_k = slice(kc * chunk, (kc + 1) * chunk)
            key_term = dot(ds_low[...], q_rows[...])
            value_term = dot(p_low[...], do_rows[...])
            acc[0, at_k, :] = acc[0, at_k, :] + key_term if add else key_term
            acc[1, at_k, :] = acc[1, at_k, :] + value_term if add else value_term
            term = dot(kv[s, 0, at_k, :], ds_low[...], ((0,), (0,)))
            dq_term = term if dq_term is None else dq_term + term
        dq_sum[...] += dq_term


    def far_block(s):
        slot = s + span // 2
        first_row = (base + s) * rows
        key_pos = lax.broadcasted_iota(jnp.int32, (piece, tile), 0).astype(F32)
        for tq in range(wide // tile):
            at_q = slice(tq * tile, (tq + 1) * tile)
            first = far_stat[2, :, at_q] - first_row.astype(F32)
            raw[tq % 2][...] = dot(kv[s, 0], qt[:, at_q])
            d_all[slot, :, at_q] = dot(kv[s, 1], dot_t[:, at_q])
            for r in range(0, rows, piece):
                at_k = slice(r, r + piece)
                scores = raw[tq % 2][at_k, :] * scale2
                e_all[slot, at_k, at_q] = jnp.where(key_pos >= first - r, scores, MASKED)
        grad_block(
            slot, s, lambda at: far_stat[0, :, at], lambda at: far_stat[1, :, at],
            far_q, far_do, far_dq, True,
        )

    turn = 2 * helps.astype(jnp.int32)

    def grad_step(i, _):
        t = xor3(span - 1 - i, turn)
        s = xor3(me, t)
        d = t // 2

        @pl.when((s <= me) & ((t < 6) | (me // 2 != 3)))
        def _():
            grad_block(
                s, s, lambda at: m_run[:, at], lambda at: w_run[:, at], qs, dos, dq_t, False
            )

            @pl.when(helps & (t == 3))
            def _():
                for i in range(3):
                    far_copy(i).wait_recv()
                far_dq[...] = jnp.zeros_like(far_dq)
                for h in range(heads):
                    at = slice(h * rows, (h + 1) * rows)
                    qt[:, at] = far_q[at, :].T
                    dot_t[:, at] = far_do[at, :].T

            @pl.when(helps & (t // 2 == 1))
            def _():
                far_block(s)

            @pl.when(helps & (t == 2))
            def _():
                far_dq_out[...] = far_dq[...].astype(BF16)
                far_copy(3).start()

            @pl.when(t == 0)
            def _():
                own[...] = acc[...]

            @pl.when(t % 2 == 1)
            def _():
                sib_out[d] = acc[...].astype(BF16)
                sib_copy(d).start()

            @pl.when((t % 2 == 0) & (t > 0))
            def _():
                sib_copy(d).wait_recv()
                acc[...] += sib_in[d].astype(F32)

            @pl.when(owns & (t == 4))
            def _():
                mid_copy.wait_recv()
                acc[...] += mid_in[...].astype(F32)

            @pl.when(t == 6)
            def _():
                mid_out[...] = acc[...].astype(BF16)
                mid_copy.start()

            @pl.when((t % 2 == 0) & (t > 0) & (t < 6))
            def _():
                red_out[d] = acc[...].astype(BF16)
                for part in (0, 1):
                    red_copy(d, part, s).start()

        return 0

    lax.fori_loop(0, span, grad_step, 0)

    @pl.when(sibling > me)
    def _():
        sib_copy(0).wait_recv()
        own[...] += sib_in[0].astype(F32)

    hd_out[0] = own[1 - side].astype(BF16)
    swap = remote(hd_out.at[0], hd_in.at[0], hd_sem.at[0], hd_sem.at[1], twin)
    swap.start()

    @pl.when(owns)
    def _():
        far_copy(3).wait_recv()
        dq_t[...] += far_dq_in[...].astype(F32)

    for h in range(heads):
        dq_ref[:, h * HDIM:(h + 1) * HDIM] = (
            (dq_t[:, h * rows:(h + 1) * rows] * scaling).T.astype(BF16)
        )

    swap.wait()
    own[side] += hd_in[0].astype(F32)

    for d, target in enumerate(partners[:2], 1):
        @pl.when(target > me)
        def _():
            for source in (0, 1):
                red_arrival(d, source).wait_recv()
                own[side] += red_in[d, source].astype(F32)

    hd_out[1] = (own[side] * jnp.where(side == 0, scaling, 1.0)).astype(BF16)
    finished = remote(hd_out.at[1], hd_in.at[1], hd_sem.at[2], hd_sem.at[3], twin)
    finished.start()
    finished.wait()

    @pl.when(side == 0)
    def _():
        dk_ref[...] = hd_out[1]
        dv_ref[...] = hd_in[1]

    @pl.when(side != 0)
    def _():
        dk_ref[...] = hd_in[1]
        dv_ref[...] = hd_out[1]

    @pl.when(sibling > me)
    def _():
        own_copy(0, sibling).wait_send()

    @pl.when(sibling < me)
    def _():
        sib_copy(0).wait_send()

    for d, target in enumerate(partners, 1):
        @pl.when(target > me)
        def _():
            own_copy(d, target).wait_send()

        @pl.when(target < me)
        def _():
            relay_copy(d, target).wait_send()
            if d < 3:
                sib_copy(d).wait_send()
                for part in (0, 1):
                    red_copy(d, part, target).wait_send()

    @pl.when(relays)
    def _():
        sib_copy(3).wait_send()
        mid_copy.wait_send()

    @pl.when(owns)
    def _():
        for i in range(3):
            far_copy(i).wait_send()

    @pl.when(helps)
    def _():
        far_copy(3).wait_send()


def copy_out(a, b, c, out_a, out_b, out_c):
    out_a[...] = a[...]
    out_b[...] = b[...]
    out_c[...] = c[...]


def body(query, keys, values, grad_out, doc_start):
    rows = keys.shape[0]
    heads = query.shape[1] // HDIM
    wide = heads * rows
    span = MAXDOC // rows
    vmem = pl.BlockSpec(memory_space=pltpu.VMEM)
    pair = (2, rows, HDIM)
    grads = pl.pallas_call(
        functools.partial(kernel, span),
        out_shape=(
            jax.ShapeDtypeStruct(query.shape, BF16),
            jax.ShapeDtypeStruct(keys.shape, BF16),
            jax.ShapeDtypeStruct(values.shape, BF16),
        ),
        in_specs=[vmem] * 5,
        out_specs=(vmem,) * 3,
        scratch_shapes=[
            pltpu.VMEM((span,) + pair, BF16),
            pltpu.VMEM((wide, HDIM), BF16),
            pltpu.VMEM((wide, HDIM), BF16),
            pltpu.VMEM((HDIM, wide), BF16),
            pltpu.VMEM((HDIM, wide), BF16),
            pltpu.VMEM((span, rows, wide), F32),
            pltpu.VMEM((span, rows, wide), F32),
            pltpu.VMEM((rows, rows // 2), F32),
            pltpu.VMEM((rows, rows // 2), F32),
            pltpu.VMEM((rows // 2, wide), BF16),
            pltpu.VMEM((rows // 2, wide), BF16),
            pltpu.VMEM((rows // 2, wide), BF16),
            pltpu.VMEM((rows // 2, wide), BF16),
            pltpu.VMEM((1, wide), F32),
            pltpu.VMEM((1, wide), F32),
            pltpu.VMEM((1, wide), F32),
            pltpu.VMEM((HDIM, wide), F32),
            pltpu.VMEM(pair, F32),
            pltpu.VMEM(pair, F32),
            pltpu.VMEM((span // 2,) + pair, BF16),
            pltpu.VMEM((span // 2,) + pair, BF16),
            pltpu.VMEM((span // 2,) + pair, BF16),
            pltpu.VMEM((span // 2,) + pair, BF16),
            pltpu.VMEM(pair, BF16),
            pltpu.VMEM(pair, BF16),
            pltpu.VMEM((wide, HDIM), BF16),
            pltpu.VMEM((wide, HDIM), BF16),
            pltpu.VMEM((3, 1, wide), F32),
            pltpu.VMEM((3, 1, wide), F32),
            pltpu.VMEM((HDIM, wide), F32),
            pltpu.VMEM((HDIM, wide), BF16),
            pltpu.VMEM((HDIM, wide), BF16),
            pltpu.VMEM(pair, BF16),
            pltpu.VMEM(pair, BF16),
            pltpu.SemaphoreType.DMA((span,)),
            pltpu.SemaphoreType.DMA((span,)),
            pltpu.SemaphoreType.DMA((span // 2,)),
            pltpu.SemaphoreType.DMA((span // 2,)),
            pltpu.SemaphoreType.DMA((span // 2, 2)),
            pltpu.SemaphoreType.DMA((span // 2, 2)),
            pltpu.SemaphoreType.DMA((4,)),
            pltpu.SemaphoreType.DMA((5,)),
            pltpu.SemaphoreType.DMA((5,)),
        ],
        compiler_params=pltpu.CompilerParams(
            collective_id=0, has_side_effects=True, vmem_limit_bytes=56 * 1024 * 1024
        ),
    )(query, keys, values, grad_out, doc_start.reshape(1, rows))
    return pl.pallas_call(
        copy_out,
        out_shape=tuple(jax.ShapeDtypeStruct(g.shape, g.dtype) for g in grads),
        in_specs=[vmem] * 3,
        out_specs=(vmem,) * 3,
        compiler_params=pltpu.CompilerParams(vmem_limit_bytes=60 * 1024 * 1024),
    )(*grads)


def solution(mesh):
    in_specs = (P("cp", "hd"), P("cp", None), P("cp", None), P("cp", "hd"), P("cp"))
    out_specs = (P("cp", "hd"), P("cp", None), P("cp", None))
    return jax.shard_map(body, mesh=mesh, in_specs=in_specs, out_specs=out_specs, check_vma=False)
```

```python
import functools
import math

import jax
import jax.numpy as jnp
from jax import lax
from jax.experimental import pallas as pl
from jax.experimental.pallas import tpu as pltpu
from jax.sharding import PartitionSpec as P

HDIM = 128
MAXDOC = 4096
MESH = pl.DeviceIdType.MESH
BF16 = jnp.bfloat16
F32 = jnp.float32
MASKED = -1e30


def xor3(a, b):
    out = 0
    for bit in (1, 2, 4):
        x, y = (a // bit) % 2, (b // bit) % 2
        out = out + bit * (x + y - 2 * x * y)
    return out


def dot(a, b, contract=((1,), (0,))):
    return lax.dot_general(a, b, (contract, ((), ())), preferred_element_type=F32)


def kernel(
    span,
    q_ref, k_ref, v_ref, do_ref, start_ref,
    dq_ref, dk_ref, dv_ref,
    kv, qs, dos, qt, dot_t, e_all, d_all, raw0, raw1, p0, p1, ds0, ds1, m_run, l_run, w_run, dq_t, acc, own,
    sib_out, sib_in, red_out, red_in, hd_out, hd_in,
    far_q, far_do, far_stat, stat_out, far_start, start_out, far_dq, far_dq_out, far_dq_in, mid_out, mid_in,
    kv_send, kv_recv, sib_send, sib_recv, red_send, red_recv, hd_sem, far_send, far_recv,
):
    rows = k_ref.shape[0]
    heads = q_ref.shape[1] // HDIM
    wide = heads * rows
    chunk = rows // 2
    tile = rows // 2
    piece = 32
    raw, p_halves, ds_halves = (raw0, raw1), (p0, p1), (ds0, ds1)
    scaling = 1.0 / math.sqrt(HDIM)
    scale2 = scaling * math.log2(math.e)

    pos = lax.axis_index("cp")
    me = pos % span
    base = pos - me
    side = lax.axis_index("hd")
    twin = {"hd": 1 - side}

    def peer(index, hd=None):
        return {"cp": base + index} if hd is None else {"cp": base + index, "hd": hd}

    sibling = xor3(me, 1)
    partners = [xor3(me, 2 * d) for d in range(1, span // 2)]

    barrier = pltpu.get_barrier_semaphore()
    greeted = [peer(sibling), twin, peer(partners[2])]
    greeted += [peer(p, hd) for p in partners[:2] for hd in (0, 1)]
    for other in greeted:
        pl.semaphore_signal(barrier, inc=1, device_id=other, device_id_type=MESH)
    pl.semaphore_wait(barrier, len(greeted))

    def remote(src, dst, send, recv, device):
        return pltpu.make_async_remote_copy(
            src_ref=src, dst_ref=dst, send_sem=send, recv_sem=recv,
            device_id=device, device_id_type=MESH,
        )

    def own_copy(d, target):
        return remote(kv.at[me], kv.at[me], kv_send.at[d], kv_recv.at[me], peer(target))

    def relay_copy(d, slot):
        return remote(
            kv.at[slot], kv.at[slot], kv_send.at[span // 2 + d], kv_recv.at[slot], peer(sibling)
        )

    def sib_copy(d):
        return remote(
            sib_out.at[d], sib_in.at[d], sib_send.at[d], sib_recv.at[d], peer(sibling)
        )

    def red_copy(d, part, target):
        return remote(
            red_out.at[d, part], red_in.at[d, side], red_send.at[d, part],
            red_recv.at[d, side], peer(target, part),
        )

    helps, relays, owns = me // 2 == 1, me // 2 == 2, me // 2 == 3
    across = peer(partners[1])

    def far_copy(i):
        src, dst = (
            (qs, far_q), (dos, far_do), (stat_out, far_stat), (far_dq_out, far_dq_in),
            (start_out, far_start),
        )[i]
        return remote(src, dst, far_send.at[i], far_recv.at[i], across)

    mid_copy = remote(mid_out, mid_in, far_send.at[5], far_recv.at[5], peer(partners[0]))

    def red_arrival(d, source):
        return remote(
            red_out.at[d, 0], red_in.at[d, source], red_send.at[d, 0],
            red_recv.at[d, source], twin,
        )

    kv[me, 0] = k_ref[...]
    kv[me, 1] = v_ref[...]
    for d, target in enumerate(partners, 1):
        @pl.when(target > me)
        def _():
            own_copy(d, target).start()

    @pl.when(sibling > me)
    def _():
        own_copy(0, sibling).start()

    for h in range(heads):
        at = slice(h * rows, (h + 1) * rows)
        q = q_ref[:, h * HDIM:(h + 1) * HDIM]
        g = do_ref[:, h * HDIM:(h + 1) * HDIM]
        qs[at, :] = q
        dos[at, :] = g
        qt[:, at] = q.T
        dot_t[:, at] = g.T

    @pl.when(owns)
    def _():
        for h in range(heads):
            start_out[:, h * rows:(h + 1) * rows] = start_ref[...].astype(F32)
        far_copy(0).start()
        far_copy(1).start()
        far_copy(4).start()

    m_run[...] = jnp.full_like(m_run, MASKED)
    l_run[...] = jnp.zeros_like(l_run)
    w_run[...] = jnp.zeros_like(w_run)
    dq_t[...] = jnp.zeros_like(dq_t)

    def load_tile(s, tq):
        at_q = slice(tq * tile, (tq + 1) * tile)
        raw[tq % 2][...] = dot(kv[s, 0], qt[:, at_q])
        d_all[s, :, at_q] = dot(kv[s, 1], dot_t[:, at_q])

    def stat_tile(s, tq, diagonal):
        at_q = slice(tq * tile, (tq + 1) * tile)
        row0 = (tq * tile) % rows
        source = raw[tq % 2]
        first = start_ref[:, row0:row0 + tile] - (base + s) * rows
        key_pos = lax.broadcasted_iota(jnp.int32, (piece, tile), 0)
        if diagonal:
            query_pos = lax.broadcasted_iota(jnp.int32, (piece, tile), 1) + row0
        old = m_run[:, at_q]
        top = jnp.broadcast_to(old, (8, tile))
        for r in range(0, rows, piece):
            at_k = slice(r, r + piece)
            allowed = key_pos >= first - r
            if diagonal:
                allowed = allowed & (key_pos + r <= query_pos)
            scores = jnp.where(allowed, source[at_k, :] * scale2, MASKED)
            e_all[s, at_k, at_q] = scores
            top = jnp.maximum(top, jnp.max(scores.reshape(piece // 8, 8, tile), axis=0))
        new = jnp.max(top, axis=0, keepdims=True)
        total = jnp.zeros((8, tile), F32)
        weighted = jnp.zeros((8, tile), F32)
        for r in range(0, rows, piece):
            at_k = slice(r, r + piece)
            e = jnp.exp2(e_all[s, at_k, at_q] - new)
            ed = e * d_all[s, at_k, at_q]
            total = total + jnp.sum(e.reshape(piece // 8, 8, tile), axis=0)
            weighted = weighted + jnp.sum(ed.reshape(piece // 8, 8, tile), axis=0)
        fac = jnp.exp2(old - new)
        l_run[:, at_q] = l_run[:, at_q] * fac + jnp.sum(total, axis=0, keepdims=True)
        w_run[:, at_q] = w_run[:, at_q] * fac + jnp.sum(weighted, axis=0, keepdims=True)
        m_run[:, at_q] = new

    def stat_block(s, diagonal):
        load_tile(s, 0)
        for tq in range(wide // tile):
            if tq + 1 < wide // tile:
                load_tile(s, tq + 1)
            stat_tile(s, tq, diagonal)

    stat_block(me, True)

    def stat_step(t, _):
        s = xor3(me, t)

        @pl.when(s < me)
        def _():
            relay_copy(0, s).wait_recv()

            @pl.when(t % 2 == 0)
            def _():
                relay_copy(t // 2, s).start()

            stat_block(s, False)

        return 0

    lax.fori_loop(1, span, stat_step, 0)

    w_run[...] = w_run[...] / l_run[...]
    m_run[...] = m_run[...] + jnp.log2(l_run[...])

    @pl.when(owns)
    def _():
        stat_out[0] = m_run[...]
        stat_out[1] = w_run[...]
        far_copy(2).start()

    def grad_block(slot, s, norm_of, delta_of, q_rows, do_rows, dq_sum, add):
        dq_term = None
        for kc in range(rows // chunk):
            p_low, ds_low = p_halves[kc], ds_halves[kc]
            for tq in range(wide // tile):
                at_q = slice(tq * tile, (tq + 1) * tile)
                norm, delta = norm_of(at_q), delta_of(at_q)
                for r in range(0, chunk, piece):
                    at_k = slice(kc * chunk + r, kc * chunk + r + piece)
                    p = jnp.exp2(e_all[slot, at_k, at_q] - norm)
                    ds = p * (d_all[slot, at_k, at_q] - delta)
                    p_low[r:r + piece, at_q] = p.astype(BF16)
                    ds_low[r:r + piece, at_q] = ds.astype(BF16)
            at_k = slice(kc * chunk, (kc + 1) * chunk)
            key_term = dot(ds_low[...], q_rows[...])
            value_term = dot(p_low[...], do_rows[...])
            acc[0, at_k, :] = acc[0, at_k, :] + key_term if add else key_term
            acc[1, at_k, :] = acc[1, at_k, :] + value_term if add else value_term
            term = dot(kv[s, 0, at_k, :], ds_low[...], ((0,), (0,)))
            dq_term = term if dq_term is None else dq_term + term
        dq_sum[...] += dq_term


    def far_scores(s):
        slot = s + span // 2
        first_row = (base + s) * rows
        key_pos = lax.broadcasted_iota(jnp.int32, (piece, tile), 0).astype(F32)
        for tq in range(wide // tile):
            at_q = slice(tq * tile, (tq + 1) * tile)
            first = far_start[:, at_q] - first_row.astype(F32)
            raw[tq % 2][...] = dot(kv[s, 0], qt[:, at_q])
            d_all[slot, :, at_q] = dot(kv[s, 1], dot_t[:, at_q])
            for r in range(0, rows, piece):
                at_k = slice(r, r + piece)
                scores = raw[tq % 2][at_k, :] * scale2
                e_all[slot, at_k, at_q] = jnp.where(key_pos >= first - r, scores, MASKED)

    def far_block(s):
        grad_block(
            s + span // 2, s, lambda at: far_stat[0, :, at], lambda at: far_stat[1, :, at],
            far_q, far_do, far_dq, True,
        )

    helping, owning = helps.astype(jnp.int32), owns.astype(jnp.int32)

    def grad_step(i, _):
        pair = i // 2
        d = 3 - pair + owning * (((pair + 1) // 2) % 2) * (2 * pair - 3)
        d = d + helping * (1 - 2 * (d % 2))
        t = 2 * d + 1 - i % 2
        s = xor3(me, t)

        @pl.when((s <= me) & ((t < 6) | (me // 2 != 3)))
        def _():
            grad_block(
                s, s, lambda at: m_run[:, at], lambda at: w_run[:, at], qs, dos, dq_t, False
            )

            @pl.when(helps & (t == 3))
            def _():
                for i in (0, 1, 4):
                    far_copy(i).wait_recv()
                far_dq[...] = jnp.zeros_like(far_dq)
                for h in range(heads):
                    at = slice(h * rows, (h + 1) * rows)
                    qt[:, at] = far_q[at, :].T
                    dot_t[:, at] = far_do[at, :].T
                far_scores(s)
                far_scores(xor3(me, 2))
                far_copy(2).wait_recv()

            @pl.when(helps & (t // 2 == 1))
            def _():
                far_block(s)

            @pl.when(helps & (t == 2))
            def _():
                far_dq_out[...] = far_dq[...].astype(BF16)
                far_copy(3).start()

            @pl.when(t == 0)
            def _():
                own[...] = acc[...]

            @pl.when(t % 2 == 1)
            def _():
                sib_out[d] = acc[...].astype(BF16)
                sib_copy(d).start()

            @pl.when((t % 2 == 0) & (t > 0))
            def _():
                sib_copy(d).wait_recv()
                acc[...] += sib_in[d].astype(F32)

            @pl.when(owns & (t == 4))
            def _():
                mid_copy.wait_recv()
                acc[...] += mid_in[...].astype(F32)

            @pl.when(t == 6)
            def _():
                mid_out[...] = acc[...].astype(BF16)
                mid_copy.start()

            @pl.when((t % 2 == 0) & (t > 0) & (t < 6))
            def _():
                red_out[d] = acc[...].astype(BF16)
                for part in (0, 1):
                    red_copy(d, part, s).start()

        return 0

    lax.fori_loop(0, span, grad_step, 0)

    @pl.when(sibling > me)
    def _():
        sib_copy(0).wait_recv()
        own[...] += sib_in[0].astype(F32)

    hd_out[0] = own[1 - side].astype(BF16)
    swap = remote(hd_out.at[0], hd_in.at[0], hd_sem.at[0], hd_sem.at[1], twin)
    swap.start()

    @pl.when(owns)
    def _():
        far_copy(3).wait_recv()
        dq_t[...] += far_dq_in[...].astype(F32)

    for h in range(heads):
        dq_ref[:, h * HDIM:(h + 1) * HDIM] = (
            (dq_t[:, h * rows:(h + 1) * rows] * scaling).T.astype(BF16)
        )

    swap.wait()
    own[side] += hd_in[0].astype(F32)

    for d, target in enumerate(partners[:2], 1):
        @pl.when(target > me)
        def _():
            for source in (0, 1):
                red_arrival(d, source).wait_recv()
                own[side] += red_in[d, source].astype(F32)

    hd_out[1] = (own[side] * jnp.where(side == 0, scaling, 1.0)).astype(BF16)
    finished = remote(hd_out.at[1], hd_in.at[1], hd_sem.at[2], hd_sem.at[3], twin)
    finished.start()
    finished.wait()

    @pl.when(side == 0)
    def _():
        dk_ref[...] = hd_out[1]
        dv_ref[...] = hd_in[1]

    @pl.when(side != 0)
    def _():
        dk_ref[...] = hd_in[1]
        dv_ref[...] = hd_out[1]

    @pl.when(sibling > me)
    def _():
        own_copy(0, sibling).wait_send()

    @pl.when(sibling < me)
    def _():
        sib_copy(0).wait_send()

    for d, target in enumerate(partners, 1):
        @pl.when(target > me)
        def _():
            own_copy(d, target).wait_send()

        @pl.when(target < me)
        def _():
            relay_copy(d, target).wait_send()
            if d < 3:
                sib_copy(d).wait_send()
                for part in (0, 1):
                    red_copy(d, part, target).wait_send()

    @pl.when(relays)
    def _():
        sib_copy(3).wait_send()
        mid_copy.wait_send()

    @pl.when(owns)
    def _():
        for i in (0, 1, 2, 4):
            far_copy(i).wait_send()

    @pl.when(helps)
    def _():
        far_copy(3).wait_send()


def copy_out(a, b, c, out_a, out_b, out_c):
    out_a[...] = a[...]
    out_b[...] = b[...]
    out_c[...] = c[...]


def body(query, keys, values, grad_out, doc_start):
    rows = keys.shape[0]
    heads = query.shape[1] // HDIM
    wide = heads * rows
    span = MAXDOC // rows
    vmem = pl.BlockSpec(memory_space=pltpu.VMEM)
    pair = (2, rows, HDIM)
    grads = pl.pallas_call(
        functools.partial(kernel, span),
        out_shape=(
            jax.ShapeDtypeStruct(query.shape, BF16),
            jax.ShapeDtypeStruct(keys.shape, BF16),
            jax.ShapeDtypeStruct(values.shape, BF16),
        ),
        in_specs=[vmem] * 5,
        out_specs=(vmem,) * 3,
        scratch_shapes=[
            pltpu.VMEM((span,) + pair, BF16),
            pltpu.VMEM((wide, HDIM), BF16),
            pltpu.VMEM((wide, HDIM), BF16),
            pltpu.VMEM((HDIM, wide), BF16),
            pltpu.VMEM((HDIM, wide), BF16),
            pltpu.VMEM((span, rows, wide), F32),
            pltpu.VMEM((span, rows, wide), F32),
            pltpu.VMEM((rows, rows // 2), F32),
            pltpu.VMEM((rows, rows // 2), F32),
            pltpu.VMEM((rows // 2, wide), BF16),
            pltpu.VMEM((rows // 2, wide), BF16),
            pltpu.VMEM((rows // 2, wide), BF16),
            pltpu.VMEM((rows // 2, wide), BF16),
            pltpu.VMEM((1, wide), F32),
            pltpu.VMEM((1, wide), F32),
            pltpu.VMEM((1, wide), F32),
            pltpu.VMEM((HDIM, wide), F32),
            pltpu.VMEM(pair, F32),
            pltpu.VMEM(pair, F32),
            pltpu.VMEM((span // 2,) + pair, BF16),
            pltpu.VMEM((span // 2,) + pair, BF16),
            pltpu.VMEM((span // 2,) + pair, BF16),
            pltpu.VMEM((span // 2,) + pair, BF16),
            pltpu.VMEM(pair, BF16),
            pltpu.VMEM(pair, BF16),
            pltpu.VMEM((wide, HDIM), BF16),
            pltpu.VMEM((wide, HDIM), BF16),
            pltpu.VMEM((2, 1, wide), F32),
            pltpu.VMEM((2, 1, wide), F32),
            pltpu.VMEM((1, wide), F32),
            pltpu.VMEM((1, wide), F32),
            pltpu.VMEM((HDIM, wide), F32),
            pltpu.VMEM((HDIM, wide), BF16),
            pltpu.VMEM((HDIM, wide), BF16),
            pltpu.VMEM(pair, BF16),
            pltpu.VMEM(pair, BF16),
            pltpu.SemaphoreType.DMA((span,)),
            pltpu.SemaphoreType.DMA((span,)),
            pltpu.SemaphoreType.DMA((span // 2,)),
            pltpu.SemaphoreType.DMA((span // 2,)),
            pltpu.SemaphoreType.DMA((span // 2, 2)),
            pltpu.SemaphoreType.DMA((span // 2, 2)),
            pltpu.SemaphoreType.DMA((4,)),
            pltpu.SemaphoreType.DMA((6,)),
            pltpu.SemaphoreType.DMA((6,)),
        ],
        compiler_params=pltpu.CompilerParams(
            collective_id=0, has_side_effects=True, vmem_limit_bytes=56 * 1024 * 1024
        ),
    )(query, keys, values, grad_out, doc_start.reshape(1, rows))
    return pl.pallas_call(
        copy_out,
        out_shape=tuple(jax.ShapeDtypeStruct(g.shape, g.dtype) for g in grads),
        in_specs=[vmem] * 3,
        out_specs=(vmem,) * 3,
        compiler_params=pltpu.CompilerParams(vmem_limit_bytes=60 * 1024 * 1024),
    )(*grads)


def solution(mesh):
    in_specs = (P("cp", "hd"), P("cp", None), P("cp", None), P("cp", "hd"), P("cp"))
    out_specs = (P("cp", "hd"), P("cp", None), P("cp", None))
    return jax.shard_map(body, mesh=mesh, in_specs=in_specs, out_specs=out_specs, check_vma=False)
```

```python
import functools
import math

import jax
import jax.numpy as jnp
from jax import lax
from jax.experimental import pallas as pl
from jax.experimental.pallas import tpu as pltpu
from jax.sharding import PartitionSpec as P

HDIM = 128
MAXDOC = 4096
MESH = pl.DeviceIdType.MESH
BF16 = jnp.bfloat16
F32 = jnp.float32
MASKED = -1e30


def xor3(a, b):
    out = 0
    for bit in (1, 2, 4):
        x, y = (a // bit) % 2, (b // bit) % 2
        out = out + bit * (x + y - 2 * x * y)
    return out


def dot(a, b, contract=((1,), (0,))):
    return lax.dot_general(a, b, (contract, ((), ())), preferred_element_type=F32)


def kernel(
    span,
    q_ref, k_ref, v_ref, do_ref, start_ref,
    dq_ref, dk_ref, dv_ref,
    kv, qs, dos, qt, dot_t, e_all, d_all, raw0, raw1, p0, p1, ds0, ds1, m_run, l_run, w_run, dq_t, acc, own,
    sib_out, sib_in, red_out, red_in, hd_out, hd_in,
    far_q, far_do, far_stat, stat_out, far_start, start_out, far_dq, far_dq_out, far_dq_in, mid_out, mid_in,
    kv_send, kv_recv, sib_send, sib_recv, red_send, red_recv, hd_sem, far_send, far_recv,
):
    rows = k_ref.shape[0]
    heads = q_ref.shape[1] // HDIM
    wide = heads * rows
    chunk = rows // 2
    tile = rows // 2
    piece = 32
    raw, p_halves, ds_halves = (raw0, raw1), (p0, p1), (ds0, ds1)
    scaling = 1.0 / math.sqrt(HDIM)
    scale2 = scaling * math.log2(math.e)

    pos = lax.axis_index("cp")
    me = pos % span
    base = pos - me
    side = lax.axis_index("hd")
    twin = {"hd": 1 - side}

    def peer(index, hd=None):
        return {"cp": base + index} if hd is None else {"cp": base + index, "hd": hd}

    sibling = xor3(me, 1)
    partners = [xor3(me, 2 * d) for d in range(1, span // 2)]

    barrier = pltpu.get_barrier_semaphore()
    greeted = [peer(sibling), twin, peer(partners[2])]
    greeted += [peer(p, hd) for p in partners[:2] for hd in (0, 1)]
    for other in greeted:
        pl.semaphore_signal(barrier, inc=1, device_id=other, device_id_type=MESH)
    pl.semaphore_wait(barrier, len(greeted))

    def remote(src, dst, send, recv, device):
        return pltpu.make_async_remote_copy(
            src_ref=src, dst_ref=dst, send_sem=send, recv_sem=recv,
            device_id=device, device_id_type=MESH,
        )

    def own_copy(d, target):
        return remote(kv.at[me], kv.at[me], kv_send.at[d], kv_recv.at[me], peer(target))

    def relay_copy(d, slot):
        return remote(
            kv.at[slot], kv.at[slot], kv_send.at[span // 2 + d], kv_recv.at[slot], peer(sibling)
        )

    def sib_copy(d):
        return remote(
            sib_out.at[d], sib_in.at[d], sib_send.at[d], sib_recv.at[d], peer(sibling)
        )

    def red_copy(d, part, target):
        return remote(
            red_out.at[d, part], red_in.at[d, side], red_send.at[d, part],
            red_recv.at[d, side], peer(target, part),
        )

    helps, relays, owns = me // 2 == 1, me // 2 == 2, me // 2 == 3
    across = peer(partners[1])

    def far_copy(i):
        src, dst = (
            (qs, far_q), (dos, far_do), (stat_out, far_stat), (far_dq_out, far_dq_in),
            (start_out, far_start),
        )[i]
        return remote(src, dst, far_send.at[i], far_recv.at[i], across)

    mid_copy = remote(mid_out, mid_in, far_send.at[5], far_recv.at[5], peer(partners[0]))

    def red_arrival(d, source):
        return remote(
            red_out.at[d, 0], red_in.at[d, source], red_send.at[d, 0],
            red_recv.at[d, source], twin,
        )

    kv[me, 0] = k_ref[...]
    kv[me, 1] = v_ref[...]
    for d, target in reversed(list(enumerate(partners, 1))):
        @pl.when(target > me)
        def _():
            own_copy(d, target).start()

    @pl.when(sibling > me)
    def _():
        own_copy(0, sibling).start()

    for h in range(heads):
        at = slice(h * rows, (h + 1) * rows)
        q = q_ref[:, h * HDIM:(h + 1) * HDIM]
        g = do_ref[:, h * HDIM:(h + 1) * HDIM]
        qs[at, :] = q
        dos[at, :] = g
        qt[:, at] = q.T
        dot_t[:, at] = g.T

    @pl.when(owns)
    def _():
        for h in range(heads):
            start_out[:, h * rows:(h + 1) * rows] = start_ref[...].astype(F32)
        far_copy(0).start()
        far_copy(1).start()
        far_copy(4).start()

    m_run[...] = jnp.full_like(m_run, MASKED)
    l_run[...] = jnp.zeros_like(l_run)
    w_run[...] = jnp.zeros_like(w_run)
    dq_t[...] = jnp.zeros_like(dq_t)

    def load_tile(s, tq):
        at_q = slice(tq * tile, (tq + 1) * tile)
        raw[tq % 2][...] = dot(kv[s, 0], qt[:, at_q])
        d_all[s, :, at_q] = dot(kv[s, 1], dot_t[:, at_q])

    def stat_tile(s, tq, diagonal):
        at_q = slice(tq * tile, (tq + 1) * tile)
        row0 = (tq * tile) % rows
        source = raw[tq % 2]
        first = start_ref[:, row0:row0 + tile] - (base + s) * rows
        key_pos = lax.broadcasted_iota(jnp.int32, (piece, tile), 0)
        if diagonal:
            query_pos = lax.broadcasted_iota(jnp.int32, (piece, tile), 1) + row0
        old = m_run[:, at_q]
        top = jnp.broadcast_to(old, (8, tile))
        for r in range(0, rows, piece):
            at_k = slice(r, r + piece)
            allowed = key_pos >= first - r
            if diagonal:
                allowed = allowed & (key_pos + r <= query_pos)
            scores = jnp.where(allowed, source[at_k, :] * scale2, MASKED)
            e_all[s, at_k, at_q] = scores
            top = jnp.maximum(top, jnp.max(scores.reshape(piece // 8, 8, tile), axis=0))
        new = jnp.max(top, axis=0, keepdims=True)
        total = jnp.zeros((8, tile), F32)
        weighted = jnp.zeros((8, tile), F32)
        for r in range(0, rows, piece):
            at_k = slice(r, r + piece)
            e = jnp.exp2(e_all[s, at_k, at_q] - new)
            ed = e * d_all[s, at_k, at_q]
            total = total + jnp.sum(e.reshape(piece // 8, 8, tile), axis=0)
            weighted = weighted + jnp.sum(ed.reshape(piece // 8, 8, tile), axis=0)
        fac = jnp.exp2(old - new)
        l_run[:, at_q] = l_run[:, at_q] * fac + jnp.sum(total, axis=0, keepdims=True)
        w_run[:, at_q] = w_run[:, at_q] * fac + jnp.sum(weighted, axis=0, keepdims=True)
        m_run[:, at_q] = new

    def stat_block(s, diagonal):
        load_tile(s, 0)
        for tq in range(wide // tile):
            if tq + 1 < wide // tile:
                load_tile(s, tq + 1)
            stat_tile(s, tq, diagonal)

    stat_block(me, True)

    def stat_step(t, _):
        s = xor3(me, t)

        @pl.when(s < me)
        def _():
            relay_copy(0, s).wait_recv()

            @pl.when(t % 2 == 0)
            def _():
                relay_copy(t // 2, s).start()

            stat_block(s, False)

        return 0

    lax.fori_loop(1, span, stat_step, 0)

    w_run[...] = w_run[...] / l_run[...]
    m_run[...] = m_run[...] + jnp.log2(l_run[...])

    @pl.when(owns)
    def _():
        stat_out[0] = m_run[...]
        stat_out[1] = w_run[...]
        far_copy(2).start()

    def grad_block(slot, s, norm_of, delta_of, q_rows, do_rows, dq_sum, add):
        dq_term = None
        for kc in range(rows // chunk):
            p_low, ds_low = p_halves[kc], ds_halves[kc]
            for tq in range(wide // tile):
                at_q = slice(tq * tile, (tq + 1) * tile)
                norm, delta = norm_of(at_q), delta_of(at_q)
                for r in range(0, chunk, piece):
                    at_k = slice(kc * chunk + r, kc * chunk + r + piece)
                    p = jnp.exp2(e_all[slot, at_k, at_q] - norm)
                    ds = p * (d_all[slot, at_k, at_q] - delta)
                    p_low[r:r + piece, at_q] = p.astype(BF16)
                    ds_low[r:r + piece, at_q] = ds.astype(BF16)
            at_k = slice(kc * chunk, (kc + 1) * chunk)
            key_term = dot(ds_low[...], q_rows[...])
            value_term = dot(p_low[...], do_rows[...])
            acc[0, at_k, :] = acc[0, at_k, :] + key_term if add else key_term
            acc[1, at_k, :] = acc[1, at_k, :] + value_term if add else value_term
            term = dot(kv[s, 0, at_k, :], ds_low[...], ((0,), (0,)))
            dq_term = term if dq_term is None else dq_term + term
        dq_sum[...] += dq_term


    def far_scores(s):
        slot = s + span // 2
        first_row = (base + s) * rows
        key_pos = lax.broadcasted_iota(jnp.int32, (piece, tile), 0).astype(F32)
        for tq in range(wide // tile):
            at_q = slice(tq * tile, (tq + 1) * tile)
            first = far_start[:, at_q] - first_row.astype(F32)
            raw[tq % 2][...] = dot(kv[s, 0], qt[:, at_q])
            d_all[slot, :, at_q] = dot(kv[s, 1], dot_t[:, at_q])
            for r in range(0, rows, piece):
                at_k = slice(r, r + piece)
                scores = raw[tq % 2][at_k, :] * scale2
                e_all[slot, at_k, at_q] = jnp.where(key_pos >= first - r, scores, MASKED)

    def far_block(s):
        grad_block(
            s + span // 2, s, lambda at: far_stat[0, :, at], lambda at: far_stat[1, :, at],
            far_q, far_do, far_dq, True,
        )

    helping, owning = helps.astype(jnp.int32), owns.astype(jnp.int32)

    def grad_step(i, _):
        pair = i // 2
        d = 3 - pair + owning * (((pair + 1) // 2) % 2) * (2 * pair - 3)
        d = d + helping * (1 - 2 * (d % 2))
        t = 2 * d + 1 - i % 2
        s = xor3(me, t)

        @pl.when((s <= me) & ((t < 6) | (me // 2 != 3)))
        def _():
            grad_block(
                s, s, lambda at: m_run[:, at], lambda at: w_run[:, at], qs, dos, dq_t, False
            )

            @pl.when(helps & (t == 3))
            def _():
                for i in (0, 1, 4):
                    far_copy(i).wait_recv()
                far_dq[...] = jnp.zeros_like(far_dq)
                for h in range(heads):
                    at = slice(h * rows, (h + 1) * rows)
                    qt[:, at] = far_q[at, :].T
                    dot_t[:, at] = far_do[at, :].T
                far_scores(s)
                far_scores(xor3(me, 2))
                far_copy(2).wait_recv()

            @pl.when(helps & (t // 2 == 1))
            def _():
                far_block(s)

            @pl.when(helps & (t == 2))
            def _():
                far_dq_out[...] = far_dq[...].astype(BF16)
                far_copy(3).start()

            @pl.when(t == 0)
            def _():
                own[...] = acc[...]

            @pl.when(t % 2 == 1)
            def _():
                sib_out[d] = acc[...].astype(BF16)
                sib_copy(d).start()

            @pl.when((t % 2 == 0) & (t > 0))
            def _():
                sib_copy(d).wait_recv()
                acc[...] += sib_in[d].astype(F32)

            @pl.when(owns & (t == 4))
            def _():
                mid_copy.wait_recv()
                acc[...] += mid_in[...].astype(F32)

            @pl.when(t == 6)
            def _():
                mid_out[...] = acc[...].astype(BF16)
                mid_copy.start()

            @pl.when((t % 2 == 0) & (t > 0) & (t < 6))
            def _():
                red_out[d] = acc[...].astype(BF16)
                for part in (1 - side, side):
                    red_copy(d, part, s).start()

        return 0

    lax.fori_loop(0, span, grad_step, 0)

    @pl.when(sibling > me)
    def _():
        sib_copy(0).wait_recv()
        own[...] += sib_in[0].astype(F32)

    hd_out[0] = own[1 - side].astype(BF16)
    swap = remote(hd_out.at[0], hd_in.at[0], hd_sem.at[0], hd_sem.at[1], twin)
    swap.start()

    @pl.when(owns)
    def _():
        far_copy(3).wait_recv()
        dq_t[...] += far_dq_in[...].astype(F32)

    for h in range(heads):
        dq_ref[:, h * HDIM:(h + 1) * HDIM] = (
            (dq_t[:, h * rows:(h + 1) * rows] * scaling).T.astype(BF16)
        )

    swap.wait()
    own[side] += hd_in[0].astype(F32)

    for d, target in enumerate(partners[:2], 1):
        @pl.when(target > me)
        def _():
            for source in (0, 1):
                red_arrival(d, source).wait_recv()
                own[side] += red_in[d, source].astype(F32)

    hd_out[1] = (own[side] * jnp.where(side == 0, scaling, 1.0)).astype(BF16)
    finished = remote(hd_out.at[1], hd_in.at[1], hd_sem.at[2], hd_sem.at[3], twin)
    finished.start()
    finished.wait()

    @pl.when(side == 0)
    def _():
        dk_ref[...] = hd_out[1]
        dv_ref[...] = hd_in[1]

    @pl.when(side != 0)
    def _():
        dk_ref[...] = hd_in[1]
        dv_ref[...] = hd_out[1]

    @pl.when(sibling > me)
    def _():
        own_copy(0, sibling).wait_send()

    @pl.when(sibling < me)
    def _():
        sib_copy(0).wait_send()

    for d, target in enumerate(partners, 1):
        @pl.when(target > me)
        def _():
            own_copy(d, target).wait_send()

        @pl.when(target < me)
        def _():
            relay_copy(d, target).wait_send()
            if d < 3:
                sib_copy(d).wait_send()
                for part in (0, 1):
                    red_copy(d, part, target).wait_send()

    @pl.when(relays)
    def _():
        sib_copy(3).wait_send()
        mid_copy.wait_send()

    @pl.when(owns)
    def _():
        for i in (0, 1, 2, 4):
            far_copy(i).wait_send()

    @pl.when(helps)
    def _():
        far_copy(3).wait_send()


def copy_out(a, b, c, out_a, out_b, out_c):
    out_a[...] = a[...]
    out_b[...] = b[...]
    out_c[...] = c[...]


def body(query, keys, values, grad_out, doc_start):
    rows = keys.shape[0]
    heads = query.shape[1] // HDIM
    wide = heads * rows
    span = MAXDOC // rows
    vmem = pl.BlockSpec(memory_space=pltpu.VMEM)
    pair = (2, rows, HDIM)
    grads = pl.pallas_call(
        functools.partial(kernel, span),
        out_shape=(
            jax.ShapeDtypeStruct(query.shape, BF16),
            jax.ShapeDtypeStruct(keys.shape, BF16),
            jax.ShapeDtypeStruct(values.shape, BF16),
        ),
        in_specs=[vmem] * 5,
        out_specs=(vmem,) * 3,
        scratch_shapes=[
            pltpu.VMEM((span,) + pair, BF16),
            pltpu.VMEM((wide, HDIM), BF16),
            pltpu.VMEM((wide, HDIM), BF16),
            pltpu.VMEM((HDIM, wide), BF16),
            pltpu.VMEM((HDIM, wide), BF16),
            pltpu.VMEM((span, rows, wide), F32),
            pltpu.VMEM((span, rows, wide), F32),
            pltpu.VMEM((rows, rows // 2), F32),
            pltpu.VMEM((rows, rows // 2), F32),
            pltpu.VMEM((rows // 2, wide), BF16),
            pltpu.VMEM((rows // 2, wide), BF16),
            pltpu.VMEM((rows // 2, wide), BF16),
            pltpu.VMEM((rows // 2, wide), BF16),
            pltpu.VMEM((1, wide), F32),
            pltpu.VMEM((1, wide), F32),
            pltpu.VMEM((1, wide), F32),
            pltpu.VMEM((HDIM, wide), F32),
            pltpu.VMEM(pair, F32),
            pltpu.VMEM(pair, F32),
            pltpu.VMEM((span // 2,) + pair, BF16),
            pltpu.VMEM((span // 2,) + pair, BF16),
            pltpu.VMEM((span // 2,) + pair, BF16),
            pltpu.VMEM((span // 2,) + pair, BF16),
            pltpu.VMEM(pair, BF16),
            pltpu.VMEM(pair, BF16),
            pltpu.VMEM((wide, HDIM), BF16),
            pltpu.VMEM((wide, HDIM), BF16),
            pltpu.VMEM((2, 1, wide), F32),
            pltpu.VMEM((2, 1, wide), F32),
            pltpu.VMEM((1, wide), F32),
            pltpu.VMEM((1, wide), F32),
            pltpu.VMEM((HDIM, wide), F32),
            pltpu.VMEM((HDIM, wide), BF16),
            pltpu.VMEM((HDIM, wide), BF16),
            pltpu.VMEM(pair, BF16),
            pltpu.VMEM(pair, BF16),
            pltpu.SemaphoreType.DMA((span,)),
            pltpu.SemaphoreType.DMA((span,)),
            pltpu.SemaphoreType.DMA((span // 2,)),
            pltpu.SemaphoreType.DMA((span // 2,)),
            pltpu.SemaphoreType.DMA((span // 2, 2)),
            pltpu.SemaphoreType.DMA((span // 2, 2)),
            pltpu.SemaphoreType.DMA((4,)),
            pltpu.SemaphoreType.DMA((6,)),
            pltpu.SemaphoreType.DMA((6,)),
        ],
        compiler_params=pltpu.CompilerParams(
            collective_id=0, has_side_effects=True, vmem_limit_bytes=56 * 1024 * 1024
        ),
    )(query, keys, values, grad_out, doc_start.reshape(1, rows))
    return pl.pallas_call(
        copy_out,
        out_shape=tuple(jax.ShapeDtypeStruct(g.shape, g.dtype) for g in grads),
        in_specs=[vmem] * 3,
        out_specs=(vmem,) * 3,
        compiler_params=pltpu.CompilerParams(vmem_limit_bytes=60 * 1024 * 1024),
    )(*grads)


def solution(mesh):
    in_specs = (P("cp", "hd"), P("cp", None), P("cp", None), P("cp", "hd"), P("cp"))
    out_specs = (P("cp", "hd"), P("cp", None), P("cp", None))
    return jax.shard_map(body, mesh=mesh, in_specs=in_specs, out_specs=out_specs, check_vma=False)
```
